256 devices in a mesh: lat: 8 (over y, x_hi), lon: 32 (over x_lo, z, core).
Axes of the slice: x: 4 (x_hi: 2, x_lo: 2; x = x_hi * 2 + x_lo), y: 4, z: 8, core: 2. Of those that a mesh axis runs over, the one named last changes fastest.
Arguments:
- features: bfloat16 [128, 384, 2048], P('lat', 'lon'), may hold values from -6 to 6
- atrous_kernel_weight: bfloat16 [9, 2048, 256], replicated, may hold values from -0.046875 to 0.046875
- point_weight: bfloat16 [2048, 256], replicated, may hold values from -0.125 to 0.125
- project_weight: bfloat16 [2, 256, 256], replicated, may hold values from -0.25 to 0.25
- upstream: bfloat16 [128, 384, 256], P('lat', 'lon'), may hold values from -6 to 6
- labels: int32 [128, 384], P('lat', 'lon'), may hold values from 0 to 2
- class_weights: float32 [3], replicated, may hold values from 0.5 to 4
Outputs:
- head_out: bfloat16 [128, 384, 256], P('lat', 'lon')
- input_grad: bfloat16 [128, 384, 2048], P('lat', 'lon')
- weight_grads: float32 [20992, 256], P('lon')
The draws below stay inside these ranges and needn't reach their ends.
All inputs are finite; a program needn't handle non-finite values.
Results may differ from the reference program's by a relative error of at most 0.006.
Values may be sent and summed in bfloat16 or wider, within the bound.
No kernel may reach another device: no remote copies, remote signals or barrier semaphores. Data moves between devices by JAX's collectives and lax.ppermute only.
A program may use at most 128 MiB of HBM per device.

```python
import math
import jax
import jax.numpy as jnp
from jax import lax

C_IN = 2048
C = 256
ATROUS_DILATION = 36
HEIGHT = 128
WIDTH = 384


def touch_ends(array, stream_key, low, top_value):
    place = [jax.random.randint(jax.random.fold_in(stream_key, axis), (), 0, length) for axis, length in enumerate(array.shape)]
    longest = array.shape.index(max(array.shape))
    next_to = place[:longest] + [(place[longest] + 1) % array.shape[longest]] + place[longest + 1:]
    return array.at[tuple(place)].set(low).at[tuple(next_to)].set(top_value)


def block_scale(stream_key, extent, cuts, smallest, largest):
    def one(axis_at, parts):
        steps = jax.random.uniform(jax.random.fold_in(jax.random.fold_in(stream_key, 6), axis_at), (parts,), jnp.float32, smallest / len(cuts), largest / len(cuts))
        return jnp.repeat(jnp.exp(steps), extent[axis_at] // parts).reshape((-1,) + (1,) * (len(extent) - axis_at - 1))

    gain = one(*cuts[0])
    for cut in cuts[1:]:
        gain = gain * one(*cut)
    return gain


def noise(rng, extent, scale, limit, cuts=(), kind=jnp.bfloat16):
    array = jax.random.normal(rng, extent, jnp.float32) * scale
    if len(cuts) > 0:
        array = block_scale(rng, extent, cuts, -0.22, 0.18) * array
    return jnp.clip(array, min=-limit, max=limit).astype(kind)


def setup_inputs(seed: int = 0) -> dict:
    key_of = jax.random.split(jax.random.key(seed), 8)
    return {
        "features": noise(key_of[0], (HEIGHT, WIDTH, C_IN), 1.0, 6.0, ((0, 8), (1, 32))),
        "atrous_kernel_weight": noise(key_of[1], (9, C_IN, C), (9 * C_IN) ** -0.5, 0.046875),
        "point_weight": noise(key_of[2], (C_IN, C), C_IN ** -0.5, 0.125),
        "project_weight": noise(key_of[3], (2, C, C), (2 * C) ** -0.5, 0.25),
        "upstream": noise(key_of[4], (HEIGHT, WIDTH, C), 1.0, 6.0, ((0, 8), (1, 32))),
        "labels": touch_ends(jax.random.randint(key_of[5], (HEIGHT, WIDTH), 0, 3), jax.random.fold_in(key_of[5], 1), 0, 2).astype(jnp.int32),
        "class_weights": jnp.clip(jnp.exp(jax.random.uniform(key_of[6], (3,), jnp.float32, math.log(0.5), math.log(4.0))), 0.5, 4.0),
    }


def spread_extent(entry_bytesize, margin):
    entry_bytesize = jnp.pad(entry_bytesize, ((0, 0), (margin, margin), (0, 0)), mode="wrap")
    return jnp.pad(entry_bytesize, ((margin, margin), (0, 0), (0, 0)))


def kernel_tap_offsets(hole_stride):
    return [(upward_direction * hole_stride, across_axis * hole_stride) for upward_direction in (-1, 0, 1) for across_axis in (-1, 0, 1)]


def contract_row_axes(left, right):
    return lax.dot_general(left, right, (((0,), (0,)), ((), ())), preferred_element_type=jnp.float32)


def multiply_transposed(left, right):
    return lax.dot_general(left, right, (((1,), (1,)), ((), ())), preferred_element_type=jnp.float32)


def silu_slope(value):
    sigmoid_value = jax.nn.sigmoid(value)
    return sigmoid_value * (1.0 + value * (1.0 - sigmoid_value))


def reference(features, atrous_kernel_weight, point_weight, project_weight, upstream, labels, class_weights):
    band_height, grid_columns, in_width = features.shape
    channel_count = point_weight.shape[1]
    padded_input = spread_extent(features, ATROUS_DILATION)

    def window_extent(entry_bytesize, margin, row_offset, column_offset):
        return entry_bytesize[margin + row_offset:margin + row_offset + band_height, margin + column_offset:margin + column_offset + grid_columns].reshape(-1, entry_bytesize.shape[-1])

    flattened = features.reshape(-1, in_width)
    point_pre = jnp.dot(flattened, point_weight, preferred_element_type=jnp.float32)
    running_total = jnp.zeros((band_height * grid_columns, channel_count), jnp.float32)
    for kernel_tap_index, (row_offset, column_offset) in enumerate(kernel_tap_offsets(ATROUS_DILATION)):
        running_total = running_total + jnp.dot(window_extent(padded_input, ATROUS_DILATION, row_offset, column_offset), atrous_kernel_weight[kernel_tap_index], preferred_element_type=jnp.float32)
    pre_list = [point_pre, running_total]
    activations = [jax.nn.silu(pre).astype(jnp.bfloat16) for pre in pre_list]
    mixed_sum = jnp.dot(activations[0], project_weight[0], preferred_element_type=jnp.float32)
    mixed_sum = mixed_sum + jnp.dot(activations[1], project_weight[1], preferred_element_type=jnp.float32)
    head_out = jax.nn.silu(mixed_sum).astype(jnp.bfloat16)
    class_index = jnp.arange(3, dtype=jnp.int32)
    pixel_weight = jnp.sum(jnp.where(labels[..., None] == class_index, class_weights, 0.0), axis=-1).reshape(-1, 1)
    out_grad = (upstream.reshape(-1, channel_count).astype(jnp.float32) * pixel_weight * silu_slope(mixed_sum)).astype(jnp.bfloat16)
    branch_gradient_list = [(multiply_transposed(out_grad, project_weight[branch]) * silu_slope(pre_list[branch])).astype(jnp.bfloat16) for branch in range(2)]
    padded_gradient = spread_extent(branch_gradient_list[1].reshape(band_height, grid_columns, channel_count), ATROUS_DILATION)
    gradient_blocks = []
    summed_input = multiply_transposed(branch_gradient_list[0], point_weight)
    for kernel_tap_index, (row_offset, column_offset) in enumerate(kernel_tap_offsets(ATROUS_DILATION)):
        gradient_blocks.append(contract_row_axes(window_extent(padded_input, ATROUS_DILATION, row_offset, column_offset), branch_gradient_list[1]))
        summed_input = summed_input + multiply_transposed(window_extent(padded_gradient, ATROUS_DILATION, -row_offset, -column_offset), atrous_kernel_weight[kernel_tap_index])
    for branch in range(2):
        gradient_blocks.append(contract_row_axes(activations[branch], out_grad))
    gradient_blocks.append(contract_row_axes(flattened, branch_gradient_list[0]))
    weight_grads = jnp.concatenate(gradient_blocks, axis=0)
    return head_out.reshape(band_height, grid_columns, channel_count), summed_input.astype(jnp.bfloat16).reshape(band_height, grid_columns, in_width), weight_grads
```

```python
import functools

import jax
import jax.numpy as jnp
from jax import lax
from jax.experimental import pallas as pl
from jax.experimental.pallas import tpu as pltpu
from jax.sharding import Mesh, PartitionSpec as P

ATROUS_DILATION = 36
LAT = ("y", "xh")
LON = ("xl", "z", "c")
AXIS_SIZES = {"y": 4, "xh": 2, "xl": 2, "z": 8, "c": 2}
LAT_COUNT = 8
LON_COUNT = 32
VMEM = pl.BlockSpec(memory_space=pltpu.VMEM)
SMEM = pl.BlockSpec(memory_space=pltpu.SMEM)
ANY = pl.BlockSpec(memory_space=pl.ANY)


def shift_rows(value, by):
    pairs = [(i, i + by) for i in range(LAT_COUNT) if 0 <= i + by < LAT_COUNT]
    return lax.ppermute(value, LAT, pairs)


def shift_columns(value, by):
    return lax.ppermute(value, LON, [(i, (i + by) % LON_COUNT) for i in range(LON_COUNT)])


def contract_row_axes(left, right):
    return lax.dot_general(
        left, right, (((0,), (0,)), ((), ())), preferred_element_type=jnp.float32
    )


def multiply_transposed(left, right):
    return lax.dot_general(
        left, right, (((1,), (1,)), ((), ())), preferred_element_type=jnp.float32
    )


def multiply(left, right):
    return jnp.dot(left, right, preferred_element_type=jnp.float32)


def sigmoid(value):
    return 1.0 / (1.0 + jnp.exp(-value))


def params(megabytes=24):
    return pltpu.CompilerParams(vmem_limit_bytes=megabytes * 2**20)


def cost(flops, moved):
    return pl.CostEstimate(flops=int(flops), bytes_accessed=int(moved), transcendentals=0)


def like(shape, dtype):
    return jax.ShapeDtypeStruct(shape, dtype)


def stream(sources, buffer_ref, semaphores):
    depth = buffer_ref.shape[0]

    def copy(at):
        return pltpu.make_async_copy(
            sources[at], buffer_ref.at[at % depth], semaphores.at[at % depth]
        )

    for at in range(min(depth - 1, len(sources))):
        copy(at).start()
    for at in range(len(sources)):
        if at + depth - 1 < len(sources):
            copy(at + depth - 1).start()
        copy(at).wait()
        yield buffer_ref.at[at % depth]


STREAM_DEPTH = 3


def stream_scratch(in_width, width):
    return [
        pltpu.VMEM((STREAM_DEPTH, in_width, width), jnp.bfloat16),
        pltpu.SemaphoreType.DMA((STREAM_DEPTH,)),
    ]


def outer_taps_kernel(
    flat_ref,
    kernel_ref,
    below_near_ref,
    below_far_ref,
    above_near_ref,
    above_far_ref,
    buffer_ref,
    semaphores,
):
    width = buffer_ref.shape[2]
    pixels = flat_ref.shape[0]
    far = below_far_ref.shape[0]
    sources = [kernel_ref.at[tap] for tap in (6, 7, 8, 0, 1, 2)]
    for at, tap_ref in enumerate(stream(sources, buffer_ref, semaphores)):
        product = multiply(flat_ref[...], tap_ref[...]).astype(jnp.bfloat16)
        lanes = slice((at % 3) * width, (at % 3 + 1) * width)
        if at < 3:
            below_far_ref[:, lanes] = product[:far]
            below_near_ref[:, lanes] = product[far:]
        else:
            above_near_ref[:, lanes] = product[: pixels - far]
            above_far_ref[:, lanes] = product[pixels - far :]


def outer_taps(flat, kernel, far):
    pixels, in_width = flat.shape
    width = kernel.shape[2]
    near_shape = like((pixels - far, 3 * width), jnp.bfloat16)
    far_shape = like((far, 3 * width), jnp.bfloat16)
    return pl.pallas_call(
        outer_taps_kernel,
        out_shape=(near_shape, far_shape, near_shape, far_shape),
        in_specs=[VMEM, ANY],
        out_specs=(VMEM,) * 4,
        scratch_shapes=stream_scratch(in_width, width),
        compiler_params=params(60),
        cost_estimate=cost(12 * pixels * in_width * width, 12 * in_width * width),
    )(flat, kernel)


def inner_taps_kernel(
    flat_ref, kernel_ref, point_weight_ref, level_ref, point_ref, buffer_ref, semaphores
):
    width = point_ref.shape[1]
    sources = [kernel_ref.at[tap] for tap in (3, 4, 5)] + [point_weight_ref]
    for at, tap_ref in enumerate(stream(sources, buffer_ref, semaphores)):
        product = multiply(flat_ref[...], tap_ref[...])
        if at < 3:
            level_ref[:, at * width : (at + 1) * width] = product
        else:
            point_ref[...] = product


def inner_taps(flat, kernel, point_weight):
    pixels, in_width = flat.shape
    width = kernel.shape[2]
    return pl.pallas_call(
        inner_taps_kernel,
        out_shape=(
            like((pixels, 3 * width), jnp.float32),
            like((pixels, width), jnp.float32),
        ),
        in_specs=[VMEM, ANY, ANY],
        out_specs=(VMEM,) * 2,
        scratch_shapes=stream_scratch(in_width, width),
        compiler_params=params(60),
        cost_estimate=cost(8 * pixels * in_width * width, 8 * in_width * width),
    )(flat, kernel, point_weight)


def slices_kernel(flat_ref, after_ref, slices_ref):
    count, _, size = slices_ref.shape
    part = size // count
    source = lax.broadcasted_iota(jnp.int32, (size, size), 0)
    target = lax.broadcasted_iota(jnp.int32, (size, size), 1)
    wanted = (source % count) * part + source // count
    picker = jnp.where(target == wanted, 1.0, 0.0).astype(jnp.bfloat16)
    sorted_blocks = [
        multiply(flat_ref[:, size * b : size * (b + 1)], picker).astype(jnp.bfloat16)
        for b in range(count)
    ]
    for a in range(count):
        slices_ref[a] = jnp.concatenate(
            [block[:, part * a : part * (a + 1)] for block in sorted_blocks], axis=1
        )


def channel_slices(flat, after):
    pixels, in_width = flat.shape
    return pl.pallas_call(
        slices_kernel,
        out_shape=like((LAT_COUNT, pixels, in_width // LAT_COUNT), jnp.bfloat16),
        in_specs=[VMEM, ANY],
        out_specs=VMEM,
        compiler_params=params(),
        cost_estimate=cost(2 * pixels * in_width * in_width // LAT_COUNT, 4 * pixels * in_width),
    )(flat, after)


def row_sum_kernel(
    level_ref,
    below_near_ref,
    below_far_ref,
    above_near_ref,
    above_far_ref,
    west_ref,
    east_ref,
    center_ref,
):
    width = center_ref.shape[1]
    near, far = below_near_ref.shape[0], below_far_ref.shape[0]
    f32 = jnp.float32
    below = jnp.concatenate([below_near_ref[...].astype(f32), below_far_ref[...].astype(f32)])
    above = jnp.concatenate([above_far_ref[...].astype(f32), above_near_ref[...].astype(f32)])
    total = level_ref[...] + below + above
    west_ref[...] = total[:, :width].astype(jnp.bfloat16)
    center_ref[...] = total[:, width : 2 * width]
    east_ref[...] = total[:, 2 * width :].astype(jnp.bfloat16)


def row_sum(level, received):
    pixels, wide = level.shape
    side = like((pixels, wide // 3), jnp.bfloat16)
    return pl.pallas_call(
        row_sum_kernel,
        out_shape=(side, side, like((pixels, wide // 3), jnp.float32)),
        in_specs=[VMEM] * 5,
        out_specs=(VMEM,) * 3,
        compiler_params=params(),
        cost_estimate=cost(3 * pixels * wide, 8 * pixels * wide),
    )(level, *received)


def head_kernel(
    point_ref,
    center_ref,
    from_east_ref,
    from_west_ref,
    project_ref,
    upstream_ref,
    pixel_weight_ref,
    after_ref,
    head_ref,
    point_grad_ref,
    atrous_grad_ref,
    message_ref,
    *terms_refs,
):
    bf16, f32 = jnp.bfloat16, jnp.float32
    count = message_ref.shape[0]
    pixels, width = point_ref.shape
    pre_list = [
        point_ref[...],
        center_ref[...] + from_east_ref[...].astype(f32) + from_west_ref[...].astype(f32),
    ]
    gates = [sigmoid(pre) for pre in pre_list]
    acts = [(pre * gate).astype(bf16) for pre, gate in zip(pre_list, gates)]
    mixed = multiply(acts[0], project_ref[0]) + multiply(acts[1], project_ref[1])
    gate = sigmoid(mixed)
    head_ref[...] = (mixed * gate).astype(bf16)
    slope = gate * (1.0 + mixed * (1.0 - gate))
    out_grad = (upstream_ref[...].astype(f32) * pixel_weight_ref[...] * slope).astype(bf16)
    grads = [
        (
            multiply_transposed(out_grad, project_ref[k])
            * (gates[k] * (1.0 + pre_list[k] * (1.0 - gates[k])))
        ).astype(bf16)
        for k in range(2)
    ]
    point_grad_ref[...] = grads[0]
    atrous_grad_ref[...] = grads[1]
    for k in range(2):
        terms = contract_row_axes(acts[k], out_grad)
        for half, terms_ref in enumerate(terms_refs):
            terms_ref[width * k : width * (k + 1), :] = terms[:, 128 * half : 128 * half + 128]
    part = 2 * width // count
    for a in range(count):
        message_ref[a, :pixels, :] = grads[1]
        message_ref[a, pixels : 2 * pixels, :] = grads[0]
        for half, terms_ref in enumerate(terms_refs):
            message_ref[a, 2 * pixels :, 128 * half : 128 * half + 128] = terms_ref[
                pl.ds(a, part, stride=count), :
            ].astype(bf16)


def head(point_pre, center, from_east, from_west, project_weight, upstream, pixel_weight, after):
    pixels, width = point_pre.shape
    field = like((pixels, width), jnp.bfloat16)
    part = 2 * width // LAT_COUNT
    return pl.pallas_call(
        head_kernel,
        out_shape=(
            field,
            field,
            field,
            like((LAT_COUNT, 2 * pixels + part, width), jnp.bfloat16),
        ),
        in_specs=[VMEM] * 7 + [ANY],
        out_specs=(VMEM,) * 4,
        scratch_shapes=[pltpu.VMEM((2 * width, 128), jnp.float32)] * (width // 128),
        compiler_params=params(),
        cost_estimate=cost(12 * pixels * width * width, 24 * pixels * width),
    )(point_pre, center, from_east, from_west, project_weight, upstream, pixel_weight, after)


def weight_terms_kernel(
    span,
    chunk,
    core_ref,
    center_ref,
    east_ref,
    west_ref,
    message_ref,
    after_east_ref,
    after_west_ref,
    kept_ref,
    sent_ref,
):
    total, width = center_ref.shape
    bands = message_ref.shape[0]
    pixels = total // bands
    room = padded(chunk)
    core = core_ref[0]
    columns = {0: center_ref, 1: east_ref, -1: west_ref}
    atrous_grad = message_ref[:, :pixels, :].reshape(total, width)
    point_grad = message_ref[:, pixels : 2 * pixels, :].reshape(total, width)

    def store(first, value):
        count = value.shape[0]
        pieces = []
        at = 0
        while at < count:
            index, offset = divmod(first + at, chunk)
            size = min(chunk - offset, count - at)
            pieces.append((index, offset, at, size))
            at += size
        for owner in (0, 1):

            @pl.when(core == owner)
            def _():
                for index, offset, at, size in pieces:
                    target = kept_ref if index % 2 == owner else sent_ref
                    first_row = index // 2 * room + offset
                    target[first_row : first_row + size, :] = value[at : at + size]

    edge = jnp.zeros((span, width), atrous_grad.dtype)
    framed = jnp.concatenate([edge, atrous_grad, edge])
    for j in (0, 1, -1):
        right = [framed[span - span * i : span - span * i + total] for i in (-1, 0, 1)]
        if j == 0:
            right.append(point_grad)
        product = contract_row_axes(columns[j][...], jnp.concatenate(right, axis=1))
        for i in (-1, 0, 1):
            store((3 * (i + 1) + j + 1) * width, product[:, (i + 1) * width : (i + 2) * width])
        if j == 0:
            project_rows = jnp.sum(message_ref[:, 2 * pixels :, :].astype(jnp.float32), axis=0)
            store(9 * width, project_rows)
            store(9 * width + project_rows.shape[0], product[:, 3 * width :])


def padded(chunk):
    return (chunk + 7) // 8 * 8


def weight_terms(span, core, center, east, west, message, after):
    total, width = center.shape
    project_rows = message.shape[1] - 2 * total // LAT_COUNT
    chunk = (10 * width + project_rows) // LON_COUNT
    out = like((LON_COUNT // 2 * padded(chunk), width), jnp.float32)
    return pl.pallas_call(
        functools.partial(weight_terms_kernel, span, chunk),
        out_shape=(out, out),
        in_specs=[SMEM] + [VMEM] * 4 + [ANY] * 2,
        out_specs=(VMEM,) * 2,
        compiler_params=params(),
        cost_estimate=cost(20 * total * width * width, 8 * 2**20),
    )(core.reshape(1), center, east, west, message, *after)


def pair_sum_kernel(kept_ref, received_ref, out_ref):
    count, chunk, _ = out_ref.shape
    room = kept_ref.shape[0] // count
    for at in range(count):
        rows = slice(room * at, room * at + chunk)
        out_ref[at] = (kept_ref[rows, :] + received_ref[rows, :]).astype(jnp.bfloat16)


def pair_sum(kept, received, chunk):
    return pl.pallas_call(
        pair_sum_kernel,
        out_shape=like((LON_COUNT // 2, chunk, kept.shape[1]), jnp.bfloat16),
        in_specs=[VMEM] * 2,
        out_specs=VMEM,
        compiler_params=params(),
        cost_estimate=cost(kept.size, 10 * kept.size),
    )(kept, received)


def piece_sum_kernel(pieces_ref, *refs):
    out_ref = refs[-1]
    total = pieces_ref[0].astype(jnp.float32)
    for at in range(1, pieces_ref.shape[0]):
        total = total + pieces_ref[at].astype(jnp.float32)
    for at in range(out_ref.shape[0]):
        out_ref[at] = total


def piece_sum(pieces, after):
    return pl.pallas_call(
        piece_sum_kernel,
        out_shape=like((LAT_COUNT,) + pieces.shape[1:], jnp.float32),
        in_specs=[VMEM] + [ANY] * len(after),
        out_specs=VMEM,
        compiler_params=params(),
        cost_estimate=cost(pieces.size, 4 * pieces.size),
    )(pieces, *after)


def interleave_kernel(parts_ref, out_ref, *sorted_refs):
    count, size, _ = parts_ref.shape
    for half, sorted_ref in enumerate(sorted_refs):
        lanes = slice(128 * half, 128 * half + 128)
        for a in range(count):
            sorted_ref[pl.ds(a, size, stride=count), :] = parts_ref[a, :, lanes]
        out_ref[:, lanes] = sorted_ref[...]


def interleave(parts):
    count, size, width = parts.shape
    return pl.pallas_call(
        interleave_kernel,
        out_shape=like((count * size, width), jnp.float32),
        in_specs=[VMEM],
        out_specs=VMEM,
        scratch_shapes=[pltpu.VMEM((count * size, 128), jnp.float32)] * (width // 128),
        compiler_params=params(),
        cost_estimate=cost(parts.size, 8 * parts.size),
    )(parts)


def center_taps_kernel(
    span,
    lat_ref,
    message_ref,
    point_grad_ref,
    east_ref,
    west_ref,
    kernel_ref,
    point_weight_ref,
    after_ref,
    total_ref,
    up_near_ref,
    up_far_ref,
    down_near_ref,
    down_far_ref,
    sides_ref,
    buffer_ref,
    semaphores,
):
    bands = message_ref.shape[0]
    pixels, width = point_grad_ref.shape
    lat = lat_ref[0]
    near = span // pixels
    far = span - near * pixels

    def part(by, low, high):
        band = lat + by
        inside = jnp.logical_and(band >= 0, band < bands)
        value = message_ref[jnp.clip(band, 0, bands - 1), low:high, :]
        return jnp.where(inside, value, jnp.zeros_like(value))

    arriving = stream(
        [point_weight_ref] + [kernel_ref.at[tap] for tap in (1, 4, 7)], buffer_ref, semaphores
    )
    for at, side_ref in enumerate((east_ref, west_ref)):
        lanes = slice(at * width, (at + 1) * width)
        side = side_ref[...]
        sides_ref[:, lanes] = side
        up_near_ref[:, lanes] = side[far:]
        up_far_ref[:, lanes] = side[:far]
        down_near_ref[:, lanes] = side[: pixels - far]
        down_far_ref[:, lanes] = side[pixels - far :]
    windows = [
        point_grad_ref[...],
        jnp.concatenate([part(near, far, pixels), part(near + 1, 0, far)]),
        message_ref[lat, :pixels, :],
        jnp.concatenate([part(-(near + 1), pixels - far, pixels), part(-near, 0, pixels - far)]),
    ]
    for at, tap_ref in enumerate(arriving):
        add_product(total_ref, windows[at], tap_ref, at == 0)


def add_product(total_ref, window, tap_ref, first):
    size = 512
    for low in range(0, total_ref.shape[1], size):
        lanes = slice(low, low + size)
        product = multiply_transposed(window, tap_ref[low : low + size, :])
        total_ref[:, lanes] = product if first else total_ref[:, lanes] + product


def center_taps(span, lat, message, point_grad, east, west, kernel, point_weight, after):
    pixels, width = point_grad.shape
    in_width = point_weight.shape[0]
    far = span % pixels
    bf16 = jnp.bfloat16
    out_shape = (
        like((pixels, in_width), jnp.float32),
        like((pixels - far, 2 * width), bf16),
        like((far, 2 * width), bf16),
        like((pixels - far, 2 * width), bf16),
        like((far, 2 * width), bf16),
        like((pixels, 2 * width), bf16),
    )
    return pl.pallas_call(
        functools.partial(center_taps_kernel, span),
        out_shape=out_shape,
        in_specs=[SMEM] + [VMEM] * 4 + [ANY] * 3,
        out_specs=(VMEM,) * 6,
        scratch_shapes=stream_scratch(in_width, width),
        compiler_params=params(60),
        cost_estimate=cost(8 * pixels * in_width * width, 12 * in_width * width),
    )(lat.reshape(1), message, point_grad, east, west, kernel, point_weight, after)


def side_taps_kernel(
    total_ref,
    sides_ref,
    up_near_ref,
    up_far_ref,
    down_near_ref,
    down_far_ref,
    kernel_ref,
    out_ref,
    sum_ref,
    buffer_ref,
    semaphores,
):
    width = buffer_ref.shape[2]
    sources = [kernel_ref.at[tap] for tap in (2, 5, 8, 0, 3, 6)]
    sum_ref[...] = total_ref[...]
    for at, tap_ref in enumerate(stream(sources, buffer_ref, semaphores)):
        side, i = divmod(at, 3)
        lanes = slice(side * width, (side + 1) * width)
        if i == 0:
            window = jnp.concatenate([up_near_ref[:, lanes], up_far_ref[:, lanes]])
        elif i == 1:
            window = sides_ref[:, lanes]
        else:
            window = jnp.concatenate([down_far_ref[:, lanes], down_near_ref[:, lanes]])
        add_product(sum_ref, window, tap_ref, False)
    out_ref[...] = sum_ref[...].astype(out_ref.dtype)


def side_taps(total, sides, received, kernel):
    pixels, in_width = total.shape
    return pl.pallas_call(
        side_taps_kernel,
        out_shape=like((pixels, in_width), jnp.bfloat16),
        in_specs=[VMEM] * 6 + [ANY],
        out_specs=VMEM,
        scratch_shapes=[pltpu.VMEM((pixels, in_width), jnp.float32)]
        + stream_scratch(in_width, kernel.shape[2]),
        compiler_params=params(60),
        cost_estimate=cost(12 * pixels * in_width * kernel.shape[2], 16 * in_width * in_width),
    )(total, sides, *received, kernel)


def shards(features, kernel, point_weight, project_weight, upstream, labels, class_weights):
    rows, cols, in_width = features.shape
    width = point_weight.shape[1]
    pixels = rows * cols
    lat_index = lax.axis_index(LAT)
    core = lax.axis_index("c")
    near = ATROUS_DILATION // rows
    far_pixels = (ATROUS_DILATION - near * rows) * cols
    tiles_over = ATROUS_DILATION // cols
    span = ATROUS_DILATION * cols

    flat = features.reshape(pixels, in_width)
    below_near, below_far, above_near, above_far = outer_taps(flat, kernel, far_pixels)
    received = (
        shift_rows(below_near, -near),
        shift_rows(below_far, -(near + 1)),
        shift_rows(above_near, near),
        shift_rows(above_far, near + 1),
    )
    level, point_pre = inner_taps(flat, kernel, point_weight)
    slices = channel_slices(flat, received[1])
    column_features = lax.all_to_all(slices, LAT, 0, 0).reshape(LAT_COUNT * pixels, -1)
    to_east, to_west, center = row_sum(level, received)
    first_east = shift_columns(column_features, -1)
    first_west = shift_columns(column_features, 1)
    from_east = shift_columns(to_west, -tiles_over)
    from_west = shift_columns(to_east, tiles_over)
    class_index = jnp.arange(3, dtype=jnp.int32)
    pixel_weight = jnp.sum(
        jnp.where(labels[..., None] == class_index, class_weights, 0.0), axis=-1
    ).reshape(-1, 1)
    head_out, point_grad, atrous_grad, message = head(
        point_pre,
        center,
        from_east,
        from_west,
        project_weight,
        upstream.reshape(pixels, width),
        pixel_weight,
        column_features,
    )

    gathered = lax.all_to_all(message, LAT, 0, 0)
    east_features = shift_columns(first_east, 1 - tiles_over)
    west_features = shift_columns(first_west, tiles_over - 1)
    east_grad = shift_columns(atrous_grad, tiles_over)
    west_grad = shift_columns(atrous_grad, -tiles_over)

    kept, sent = weight_terms(
        span, core, column_features, east_features, west_features, gathered, (east_grad, west_grad)
    )
    chunk = (10 * in_width + 2 * width) // (LAT_COUNT * LON_COUNT)
    chip_sum = pair_sum(kept, lax.ppermute(sent, "c", [(0, 1), (1, 0)]), chunk)
    pieces = lax.all_to_all(chip_sum, ("xl", "z"), 0, 0)

    total, up_near, up_far, down_near, down_far, sides = center_taps(
        span, lat_index, gathered, point_grad, east_grad, west_grad, kernel, point_weight, chip_sum
    )
    side_rows = (
        shift_rows(up_near, -near),
        shift_rows(up_far, -(near + 1)),
        shift_rows(down_near, near),
        shift_rows(down_far, near + 1),
    )
    weight_grads = interleave(lax.all_to_all(piece_sum(pieces, side_rows), LAT, 0, 0))
    summed_input = side_taps(total, sides, side_rows, kernel)

    head_tile = head_out.reshape(rows, cols, width)
    grad_tile = summed_input.reshape(rows, cols, in_width)
    return (head_tile, grad_tile, weight_grads)


def solution(mesh):
    split = Mesh(mesh.devices.reshape(tuple(AXIS_SIZES.values())), tuple(AXIS_SIZES))
    tile = P(LAT, LON, None)
    return jax.shard_map(
        shards,
        mesh=split,
        in_specs=(tile, P(), P(), P(), tile, P(LAT, LON), P()),
        out_specs=(tile, tile, P(LON, None)),
        check_vma=False,
    )
```

```python
import functools

import jax
import jax.numpy as jnp
from jax import lax
from jax.experimental import pallas as pl
from jax.experimental.pallas import tpu as pltpu
from jax.sharding import Mesh, PartitionSpec as P

ATROUS_DILATION = 36
LAT = ("y", "xh")
LON = ("xl", "z", "c")
AXIS_SIZES = {"y": 4, "xh": 2, "xl": 2, "z": 8, "c": 2}
LAT_COUNT = 8
LON_COUNT = 32
VMEM = pl.BlockSpec(memory_space=pltpu.VMEM)
SMEM = pl.BlockSpec(memory_space=pltpu.SMEM)
ANY = pl.BlockSpec(memory_space=pl.ANY)


def shift_rows(value, by):
    pairs = [(i, i + by) for i in range(LAT_COUNT) if 0 <= i + by < LAT_COUNT]
    return lax.ppermute(value, LAT, pairs)


def shift_columns(value, by):
    return lax.ppermute(value, LON, [(i, (i + by) % LON_COUNT) for i in range(LON_COUNT)])


def contract_row_axes(left, right):
    return lax.dot_general(
        left, right, (((0,), (0,)), ((), ())), preferred_element_type=jnp.float32
    )


def multiply_transposed(left, right):
    return lax.dot_general(
        left, right, (((1,), (1,)), ((), ())), preferred_element_type=jnp.float32
    )


def multiply(left, right):
    return jnp.dot(left, right, preferred_element_type=jnp.float32)


def sigmoid(value):
    return 1.0 / (1.0 + jnp.exp(-value))


def params(megabytes=24):
    return pltpu.CompilerParams(vmem_limit_bytes=megabytes * 2**20)


def cost(flops, moved):
    return pl.CostEstimate(flops=int(flops), bytes_accessed=int(moved), transcendentals=0)


def like(shape, dtype):
    return jax.ShapeDtypeStruct(shape, dtype)


def stream(sources, buffer_ref, semaphores):
    depth = buffer_ref.shape[0]

    def copy(at):
        return pltpu.make_async_copy(
            sources[at], buffer_ref.at[at % depth], semaphores.at[at % depth]
        )

    for at in range(min(depth - 1, len(sources))):
        copy(at).start()
    for at in range(len(sources)):
        if at + depth - 1 < len(sources):
            copy(at + depth - 1).start()
        copy(at).wait()
        yield buffer_ref.at[at % depth]


STREAM_DEPTH = 3


def stream_scratch(in_width, width):
    return [
        pltpu.VMEM((STREAM_DEPTH, in_width, width), jnp.bfloat16),
        pltpu.SemaphoreType.DMA((STREAM_DEPTH,)),
    ]


def products_kernel(
    flat_ref,
    kernel_ref,
    point_weight_ref,
    after_ref,
    below_near_ref,
    below_far_ref,
    above_near_ref,
    above_far_ref,
    level_ref,
    point_ref,
):
    width = kernel_ref.shape[2]
    pixels = flat_ref.shape[0]
    far = below_far_ref.shape[0]
    for at, tap in enumerate((6, 7, 8, 0, 1, 2, 3, 4, 5)):
        product = multiply(flat_ref[...], kernel_ref[tap])
        rounded = product.astype(jnp.bfloat16)
        lanes = slice((at % 3) * width, (at % 3 + 1) * width)
        if at < 3:
            below_far_ref[:, lanes] = rounded[:far]
            below_near_ref[:, lanes] = rounded[far:]
        elif at < 6:
            above_near_ref[:, lanes] = rounded[: pixels - far]
            above_far_ref[:, lanes] = rounded[pixels - far :]
        else:
            level_ref[:, lanes] = product
    point_ref[...] = multiply(flat_ref[...], point_weight_ref[...])


def tap_products(flat, kernel, point_weight, far, after):
    pixels, in_width = flat.shape
    width = kernel.shape[2]
    near_shape = like((pixels - far, 3 * width), jnp.bfloat16)
    far_shape = like((far, 3 * width), jnp.bfloat16)
    return pl.pallas_call(
        products_kernel,
        out_shape=(near_shape, far_shape, near_shape, far_shape)
        + (like((pixels, 3 * width), jnp.float32), like((pixels, width), jnp.float32)),
        in_specs=[VMEM] * 3 + [ANY],
        out_specs=(VMEM,) * 6,
        compiler_params=params(),
        cost_estimate=cost(20 * pixels * in_width * width, 20 * in_width * width),
    )(flat, kernel, point_weight, after)


def slices_kernel(flat_ref, slices_ref):
    count, _, size = slices_ref.shape
    part = size // count
    source = lax.broadcasted_iota(jnp.int32, (size, size), 0)
    target = lax.broadcasted_iota(jnp.int32, (size, size), 1)
    wanted = (source % count) * part + source // count
    picker = jnp.where(target == wanted, 1.0, 0.0).astype(jnp.bfloat16)
    sorted_blocks = [
        multiply(flat_ref[:, size * b : size * (b + 1)], picker).astype(jnp.bfloat16)
        for b in range(count)
    ]
    for a in range(count):
        slices_ref[a] = jnp.concatenate(
            [block[:, part * a : part * (a + 1)] for block in sorted_blocks], axis=1
        )


def channel_slices(flat):
    pixels, in_width = flat.shape
    return pl.pallas_call(
        slices_kernel,
        out_shape=like((LAT_COUNT, pixels, in_width // LAT_COUNT), jnp.bfloat16),
        in_specs=[VMEM],
        out_specs=VMEM,
        compiler_params=params(),
        cost_estimate=cost(10**10, 4 * pixels * in_width),
    )(flat)


def row_sum_kernel(
    level_ref,
    below_near_ref,
    below_far_ref,
    above_near_ref,
    above_far_ref,
    features_in_ref,
    west_ref,
    east_ref,
    center_ref,
    features_out_ref,
):
    width = center_ref.shape[1]
    near, far = below_near_ref.shape[0], below_far_ref.shape[0]
    f32 = jnp.float32
    below = jnp.concatenate([below_near_ref[...].astype(f32), below_far_ref[...].astype(f32)])
    above = jnp.concatenate([above_far_ref[...].astype(f32), above_near_ref[...].astype(f32)])
    total = level_ref[...] + below + above
    west_ref[...] = total[:, :width].astype(jnp.bfloat16)
    center_ref[...] = total[:, width : 2 * width]
    east_ref[...] = total[:, 2 * width :].astype(jnp.bfloat16)


def row_sum(level, received, features):
    pixels, wide = level.shape
    side = like((pixels, wide // 3), jnp.bfloat16)
    return pl.pallas_call(
        row_sum_kernel,
        out_shape=(
            side,
            side,
            like((pixels, wide // 3), jnp.float32),
            like(features.shape, features.dtype),
        ),
        in_specs=[VMEM] * 5 + [ANY],
        out_specs=(VMEM,) * 3 + (ANY,),
        input_output_aliases={5: 3},
        compiler_params=params(),
        cost_estimate=cost(3 * pixels * wide, 8 * pixels * wide),
    )(level, *received, features)


def head_kernel(
    point_ref,
    center_ref,
    from_east_ref,
    from_west_ref,
    project_ref,
    upstream_ref,
    pixel_weight_ref,
    after_east_ref,
    after_west_ref,
    head_ref,
    grads_ref,
    message_ref,
    *terms_refs,
):
    bf16, f32 = jnp.bfloat16, jnp.float32
    width = point_ref.shape[1]
    pre_list = [
        point_ref[...],
        center_ref[...] + from_east_ref[...].astype(f32) + from_west_ref[...].astype(f32),
    ]
    gates = [sigmoid(pre) for pre in pre_list]
    acts = [(pre * gate).astype(bf16) for pre, gate in zip(pre_list, gates)]
    mixed = multiply(acts[0], project_ref[0]) + multiply(acts[1], project_ref[1])
    gate = sigmoid(mixed)
    head_ref[...] = (mixed * gate).astype(bf16)
    slope = gate * (1.0 + mixed * (1.0 - gate))
    out_grad = (upstream_ref[...].astype(f32) * pixel_weight_ref[...] * slope).astype(bf16)
    grads = [
        (
            multiply_transposed(out_grad, project_ref[k])
            * (gates[k] * (1.0 + pre_list[k] * (1.0 - gates[k])))
        ).astype(bf16)
        for k in range(2)
    ]
    pixels = grads_ref.shape[0]
    grads_ref[:, :width] = grads[1]
    grads_ref[:, width:] = grads[0]
    for k in range(2):
        terms = contract_row_axes(acts[k], out_grad)
        for half, terms_ref in enumerate(terms_refs):
            terms_ref[width * k : width * (k + 1), :] = terms[:, 128 * half : 128 * half + 128]
    count = message_ref.shape[0]
    part = 2 * width // count
    for a in range(count):
        message_ref[a, :pixels, :] = grads[1]
        message_ref[a, pixels : 2 * pixels, :] = grads[0]
        for half, terms_ref in enumerate(terms_refs):
            message_ref[a, 2 * pixels :, 128 * half : 128 * half + 128] = terms_ref[
                pl.ds(a, part, stride=count), :
            ].astype(bf16)


def head(point_pre, center, from_east, from_west, project, upstream, pixel_weight, after):
    pixels, width = point_pre.shape
    part = 2 * width // LAT_COUNT
    bf16, f32 = jnp.bfloat16, jnp.float32
    return pl.pallas_call(
        head_kernel,
        out_shape=(
            like((pixels, width), bf16),
            like((pixels, 2 * width), bf16),
            like((LAT_COUNT, 2 * pixels + part, width), bf16),
        ),
        in_specs=[VMEM] * 7 + [ANY] * 2,
        out_specs=(VMEM,) * 3,
        scratch_shapes=[pltpu.VMEM((2 * width, 128), f32)] * (width // 128),
        compiler_params=params(),
        cost_estimate=cost(12 * pixels * width * width, 24 * pixels * width),
    )(point_pre, center, from_east, from_west, project, upstream, pixel_weight, *after)


def weight_terms_kernel(
    span,
    chunk,
    place_ref,
    center_ref,
    east_first_ref,
    west_first_ref,
    east_second_ref,
    west_second_ref,
    message_ref,
    east_grad_ref,
    west_grad_ref,
    kept_ref,
    sent_ref,
    windows_ref,
    up_near_ref,
    up_far_ref,
    down_near_ref,
    down_far_ref,
    framed_ref,
):
    total, width = center_ref.shape
    pixels = total // LAT_COUNT
    room = padded(chunk)
    core, lat = place_ref[0], place_ref[1]
    far = up_far_ref.shape[0]
    columns = {
        0: (center_ref,),
        1: (east_first_ref, east_second_ref),
        -1: (west_first_ref, west_second_ref),
    }

    edge = jnp.zeros((span, width), framed_ref.dtype)
    framed_ref[total : total + span, :width] = edge
    framed_ref[span : 2 * span, 2 * width : 3 * width] = edge
    for band in range(LAT_COUNT):
        piece = message_ref[band, :pixels, :]
        for i in (-1, 0, 1):
            first = span + span * i + band * pixels
            framed_ref[first : first + pixels, (i + 1) * width : (i + 2) * width] = piece
        first = span + band * pixels
        framed_ref[first : first + pixels, 3 * width :] = message_ref[band, pixels : 2 * pixels, :]
    for at, side_ref in enumerate((east_grad_ref, west_grad_ref)):
        lanes = slice(at * width, (at + 1) * width)
        side = side_ref[...]
        up_near_ref[:, lanes] = side[far:]
        up_far_ref[:, lanes] = side[:far]
        down_near_ref[:, lanes] = side[: pixels - far]
        down_far_ref[:, lanes] = side[pixels - far :]
    own_rows = pl.ds(pl.multiple_of(span + lat * pixels, 16), pixels)
    windows_ref[...] = framed_ref[own_rows, : 3 * width]

    def store(first, value):
        count = value.shape[0]
        pieces = []
        at = 0
        while at < count:
            index, offset = divmod(first + at, chunk)
            size = min(chunk - offset, count - at)
            pieces.append((index, offset, at, size))
            at += size
        for owner in (0, 1):

            @pl.when(core == owner)
            def _():
                for index, offset, at, size in pieces:
                    target = kept_ref if index % 2 == owner else sent_ref
                    first_row = index // 2 * room + offset
                    target[first_row : first_row + size, :] = value[at : at + size]

    for j in (0, 1, -1):
        wide = 4 * width if j == 0 else 3 * width
        product, low = 0.0, span
        for part_ref in columns[j]:
            high = low + part_ref.shape[0]
            product += contract_row_axes(part_ref[...], framed_ref[low:high, :wide])
            low = high
        for i in (-1, 0, 1):
            store((3 * (i + 1) + j + 1) * width, product[:, (i + 1) * width : (i + 2) * width])
        if j == 0:
            project_rows = jnp.sum(message_ref[:, 2 * pixels :, :].astype(jnp.float32), axis=0)
            store(9 * width, project_rows)
            store(9 * width + project_rows.shape[0], product[:, 3 * width :])


def padded(chunk):
    return (chunk + 7) // 8 * 8


def weight_terms(span, place, features, message, sides):
    total, width = features[0].shape
    pixels = total // LAT_COUNT
    far = span % pixels
    chunk = (10 * width + message.shape[1] - 2 * pixels) // LON_COUNT
    out = like((LON_COUNT // 2 * padded(chunk), width), jnp.float32)
    near_shape = like((pixels - far, 2 * width), jnp.bfloat16)
    far_shape = like((far, 2 * width), jnp.bfloat16)
    return pl.pallas_call(
        functools.partial(weight_terms_kernel, span, chunk),
        out_shape=(out, out, like((pixels, 3 * width), jnp.bfloat16))
        + (near_shape, far_shape, near_shape, far_shape),
        in_specs=[SMEM] + [VMEM] * 8,
        out_specs=(VMEM,) * 7,
        scratch_shapes=[pltpu.VMEM((2 * span + total, 4 * width), jnp.bfloat16)],
        compiler_params=params(),
        cost_estimate=cost(20 * total * width * width, 8 * 2**20),
    )(place, *features, message, *sides)


def pair_sum_kernel(kept_ref, received_ref, out_ref):
    count, chunk, _ = out_ref.shape
    room = kept_ref.shape[0] // count
    for at in range(count):
        rows = slice(room * at, room * at + chunk)
        out_ref[at] = (kept_ref[rows, :] + received_ref[rows, :]).astype(jnp.bfloat16)


def pair_sum(kept, received, chunk):
    return pl.pallas_call(
        pair_sum_kernel,
        out_shape=like((LON_COUNT // 2, chunk, kept.shape[1]), jnp.bfloat16),
        in_specs=[VMEM] * 2,
        out_specs=VMEM,
        compiler_params=params(),
        cost_estimate=cost(kept.size, 10 * kept.size),
    )(kept, received)


def piece_sum_kernel(pieces_ref, *refs):
    out_ref = refs[-1]
    total = pieces_ref[0].astype(jnp.float32)
    for at in range(1, pieces_ref.shape[0]):
        total = total + pieces_ref[at].astype(jnp.float32)
    for at in range(out_ref.shape[0]):
        out_ref[at] = total


def piece_sum(pieces, after):
    return pl.pallas_call(
        piece_sum_kernel,
        out_shape=like((LAT_COUNT,) + pieces.shape[1:], jnp.float32),
        in_specs=[VMEM] + [ANY] * len(after),
        out_specs=VMEM,
        compiler_params=params(),
        cost_estimate=cost(pieces.size, 4 * pieces.size),
    )(pieces, *after)


def interleave_kernel(parts_ref, out_ref, *sorted_refs):
    count, size, _ = parts_ref.shape
    for half, sorted_ref in enumerate(sorted_refs):
        lanes = slice(128 * half, 128 * half + 128)
        for a in range(count):
            sorted_ref[pl.ds(a, size, stride=count), :] = parts_ref[a, :, lanes]
        out_ref[:, lanes] = sorted_ref[...]


def interleave(parts):
    count, size, width = parts.shape
    return pl.pallas_call(
        interleave_kernel,
        out_shape=like((count * size, width), jnp.float32),
        in_specs=[VMEM],
        out_specs=VMEM,
        scratch_shapes=[pltpu.VMEM((count * size, 128), jnp.float32)] * (width // 128),
        compiler_params=params(),
        cost_estimate=cost(parts.size, 8 * parts.size),
    )(parts)


def add_product(total_ref, window, tap_ref, first):
    size = 512
    for low in range(0, total_ref.shape[1], size):
        lanes = slice(low, low + size)
        product = multiply_transposed(window, tap_ref[low : low + size, :])
        total_ref[:, lanes] = product if first else total_ref[:, lanes] + product


def input_gradient_kernel(
    windows_ref,
    grads_ref,
    east_ref,
    west_ref,
    up_near_ref,
    up_far_ref,
    down_near_ref,
    down_far_ref,
    kernel_ref,
    point_weight_ref,
    out_ref,
    total_ref,
    buffer_ref,
    semaphores,
):
    width = buffer_ref.shape[2]
    sources = [point_weight_ref] + [kernel_ref.at[tap] for tap in (1, 4, 7, 2, 5, 8, 0, 3, 6)]
    for at, tap_ref in enumerate(stream(sources, buffer_ref, semaphores)):
        side, i = divmod(at - 4, 3)
        lanes = slice(side * width, (side + 1) * width)
        if at == 0:
            window = grads_ref[:, width:]
        elif at < 4:
            window = windows_ref[:, (at - 1) * width : at * width]
        elif i == 0:
            window = jnp.concatenate([up_near_ref[:, lanes], up_far_ref[:, lanes]])
        elif i == 1:
            window = (east_ref, west_ref)[side][...]
        else:
            window = jnp.concatenate([down_far_ref[:, lanes], down_near_ref[:, lanes]])
        add_product(total_ref, window, tap_ref, at == 0)
    out_ref[...] = total_ref[...].astype(out_ref.dtype)


def input_gradient(windows, grads, east, west, side_rows, kernel, point_weight):
    pixels = grads.shape[0]
    in_width, width = point_weight.shape
    return pl.pallas_call(
        input_gradient_kernel,
        out_shape=like((pixels, in_width), jnp.bfloat16),
        in_specs=[VMEM] * 8 + [ANY] * 2,
        out_specs=VMEM,
        scratch_shapes=[pltpu.VMEM((pixels, in_width), jnp.float32)]
        + stream_scratch(in_width, width),
        compiler_params=params(60),
        cost_estimate=cost(20 * pixels * in_width * width, 40 * in_width * width),
    )(windows, grads, east, west, *side_rows, kernel, point_weight)


def shards(features, kernel, point_weight, project_weight, upstream, labels, class_weights):
    rows, cols, in_width = features.shape
    width = point_weight.shape[1]
    pixels = rows * cols
    place = jnp.stack([lax.axis_index("c"), lax.axis_index(LAT)])
    near = ATROUS_DILATION // rows
    far_pixels = (ATROUS_DILATION - near * rows) * cols
    tiles_over = ATROUS_DILATION // cols
    span = ATROUS_DILATION * cols

    flat = features.reshape(pixels, in_width)
    slices = channel_slices(flat)
    below_near, below_far, above_near, above_far, level, point_pre = tap_products(
        flat, kernel, point_weight, far_pixels, slices
    )
    received = (
        shift_rows(below_near, -near),
        shift_rows(below_far, -(near + 1)),
        shift_rows(above_near, near),
        shift_rows(above_far, near + 1),
    )
    column_features = lax.all_to_all(slices, LAT, 0, 0).reshape(LAT_COUNT * pixels, -1)
    half = LAT_COUNT // 2 * pixels
    first_half, second_half = column_features[:half], column_features[half:]
    to_east, to_west, center, first_half = row_sum(level, received, first_half)
    first_east = shift_columns(first_half, -tiles_over)
    first_west = shift_columns(first_half, tiles_over)
    from_east = shift_columns(to_west, -tiles_over)
    from_west = shift_columns(to_east, tiles_over)
    class_index = jnp.arange(3, dtype=jnp.int32)
    pixel_weight = jnp.sum(
        jnp.where(labels[..., None] == class_index, class_weights, 0.0), axis=-1
    ).reshape(-1, 1)
    head_out, grads, message = head(
        point_pre,
        center,
        from_east,
        from_west,
        project_weight,
        upstream.reshape(pixels, width),
        pixel_weight,
        (first_east, first_west),
    )

    gathered = lax.all_to_all(message, LAT, 0, 0)
    second_east = shift_columns(second_half, -tiles_over)
    second_west = shift_columns(second_half, tiles_over)
    east_grad = shift_columns(grads[:, :width], tiles_over)
    west_grad = shift_columns(grads[:, :width], -tiles_over)

    kept, sent, windows, up_near, up_far, down_near, down_far = weight_terms(
        span,
        place,
        (column_features, first_east, first_west, second_east, second_west),
        gathered,
        (east_grad, west_grad),
    )
    side_rows = (
        shift_rows(up_near, -near),
        shift_rows(up_far, -(near + 1)),
        shift_rows(down_near, near),
        shift_rows(down_far, near + 1),
    )
    chunk = (10 * in_width + 2 * width) // (LAT_COUNT * LON_COUNT)
    chip_sum = pair_sum(kept, lax.ppermute(sent, "c", [(0, 1), (1, 0)]), chunk)
    pieces = lax.all_to_all(chip_sum, ("xl", "z"), 0, 0)

    weight_grads = interleave(lax.all_to_all(piece_sum(pieces, side_rows), LAT, 0, 0))
    summed_input = input_gradient(
        windows, grads, east_grad, west_grad, side_rows, kernel, point_weight
    )

    head_tile = head_out.reshape(rows, cols, width)
    grad_tile = summed_input.reshape(rows, cols, in_width)
    return (head_tile, grad_tile, weight_grads)


def solution(mesh):
    split = Mesh(mesh.devices.reshape(tuple(AXIS_SIZES.values())), tuple(AXIS_SIZES))
    tile = P(LAT, LON, None)
    return jax.shard_map(
        shards,
        mesh=split,
        in_specs=(tile, P(), P(), P(), tile, P(LAT, LON), P()),
        out_specs=(tile, tile, P(LON, None)),
        check_vma=False,
    )
```

```python
import functools

import jax
import jax.numpy as jnp
from jax import lax
from jax.experimental import pallas as pl
from jax.experimental.pallas import tpu as pltpu
from jax.sharding import Mesh, PartitionSpec as P

ATROUS_DILATION = 36
LAT = ("y", "xh")
LON = ("xl", "z", "c")
AXIS_SIZES = {"y": 4, "xh": 2, "xl": 2, "z": 8, "c": 2}
LAT_COUNT = 8
LON_COUNT = 32
FIRST_BANDS = 4
VMEM = pl.BlockSpec(memory_space=pltpu.VMEM)
SMEM = pl.BlockSpec(memory_space=pltpu.SMEM)
ANY = pl.BlockSpec(memory_space=pl.ANY)


def shift_rows(value, by):
    pairs = [(i, i + by) for i in range(LAT_COUNT) if 0 <= i + by < LAT_COUNT]
    return lax.ppermute(value, LAT, pairs)


def shift_columns(value, by):
    return lax.ppermute(value, LON, [(i, (i + by) % LON_COUNT) for i in range(LON_COUNT)])


def contract_row_axes(left, right):
    return lax.dot_general(
        left, right, (((0,), (0,)), ((), ())), preferred_element_type=jnp.float32
    )


def multiply_transposed(left, right):
    return lax.dot_general(
        left, right, (((1,), (1,)), ((), ())), preferred_element_type=jnp.float32
    )


def multiply(left, right):
    return jnp.dot(left, right, preferred_element_type=jnp.float32)


def sigmoid(value):
    return 1.0 / (1.0 + jnp.exp(-value))


def params(megabytes=24):
    return pltpu.CompilerParams(vmem_limit_bytes=megabytes * 2**20)


def cost(flops, moved):
    return pl.CostEstimate(flops=int(flops), bytes_accessed=int(moved), transcendentals=0)


def like(shape, dtype):
    return jax.ShapeDtypeStruct(shape, dtype)


def stream(sources, buffer_ref, semaphores):
    depth = buffer_ref.shape[0]

    def copy(at):
        return pltpu.make_async_copy(
            sources[at], buffer_ref.at[at % depth], semaphores.at[at % depth]
        )

    for at in range(min(depth - 1, len(sources))):
        copy(at).start()
    for at in range(len(sources)):
        if at + depth - 1 < len(sources):
            copy(at + depth - 1).start()
        copy(at).wait()
        yield buffer_ref.at[at % depth]


STREAM_DEPTH = 3


def stream_scratch(in_width, width):
    return [
        pltpu.VMEM((STREAM_DEPTH, in_width, width), jnp.bfloat16),
        pltpu.SemaphoreType.DMA((STREAM_DEPTH,)),
    ]


def products_kernel(
    flat_ref,
    kernel_ref,
    point_weight_ref,
    after_ref,
    below_near_ref,
    below_far_ref,
    above_near_ref,
    above_far_ref,
    level_ref,
    point_ref,
):
    width = kernel_ref.shape[2]
    pixels = flat_ref.shape[0]
    far = below_far_ref.shape[0]
    for at, tap in enumerate((6, 7, 8, 0, 1, 2, 3, 4, 5)):
        product = multiply(flat_ref[...], kernel_ref[tap])
        rounded = product.astype(jnp.bfloat16)
        lanes = slice((at % 3) * width, (at % 3 + 1) * width)
        if at < 3:
            below_far_ref[:, lanes] = rounded[:far]
            below_near_ref[:, lanes] = rounded[far:]
        elif at < 6:
            above_near_ref[:, lanes] = rounded[: pixels - far]
            above_far_ref[:, lanes] = rounded[pixels - far :]
        else:
            level_ref[:, lanes] = product
    point_ref[...] = multiply(flat_ref[...], point_weight_ref[...])


def tap_products(flat, kernel, point_weight, far, after):
    pixels, in_width = flat.shape
    width = kernel.shape[2]
    near_shape = like((pixels - far, 3 * width), jnp.bfloat16)
    far_shape = like((far, 3 * width), jnp.bfloat16)
    return pl.pallas_call(
        products_kernel,
        out_shape=(near_shape, far_shape, near_shape, far_shape)
        + (like((pixels, 3 * width), jnp.float32), like((pixels, width), jnp.float32)),
        in_specs=[VMEM] * 3 + [ANY],
        out_specs=(VMEM,) * 6,
        compiler_params=params(),
        cost_estimate=cost(20 * pixels * in_width * width, 20 * in_width * width),
    )(flat, kernel, point_weight, after)


def slices_kernel(columns_ref, flat_ref, slices_ref, *row_refs):
    cols, rows, _ = columns_ref.shape
    for block, row_ref in enumerate(row_refs):
        lanes = slice(128 * block, 128 * block + 128)
        for col in range(cols):
            row_ref[pl.ds(col, rows, stride=cols), :] = columns_ref[col, :, lanes].astype(
                jnp.float32
            )
        flat_ref[:, lanes] = row_ref[...].astype(jnp.bfloat16)
    count, _, size = slices_ref.shape
    part = size // count
    source = lax.broadcasted_iota(jnp.int32, (size, size), 0)
    target = lax.broadcasted_iota(jnp.int32, (size, size), 1)
    wanted = (source % count) * part + source // count
    picker = jnp.where(target == wanted, 1.0, 0.0).astype(jnp.bfloat16)
    sorted_blocks = [
        multiply(flat_ref[:, size * b : size * (b + 1)], picker).astype(jnp.bfloat16)
        for b in range(count)
    ]
    for a in range(count):
        slices_ref[a] = jnp.concatenate(
            [block[:, part * a : part * (a + 1)] for block in sorted_blocks], axis=1
        )


def channel_slices(features):
    rows, cols, in_width = features.shape
    pixels = rows * cols
    return pl.pallas_call(
        slices_kernel,
        out_shape=(
            like((pixels, in_width), jnp.bfloat16),
            like((LAT_COUNT, pixels, in_width // LAT_COUNT), jnp.bfloat16),
        ),
        in_specs=[VMEM],
        out_specs=(VMEM,) * 2,
        scratch_shapes=[pltpu.VMEM((pixels, 128), jnp.float32)] * (in_width // 128),
        compiler_params=params(),
        cost_estimate=cost(2 * pixels * in_width * in_width // LAT_COUNT, 6 * pixels * in_width),
    )(jnp.swapaxes(features, 0, 1))


def row_sum_kernel(
    level_ref,
    below_near_ref,
    below_far_ref,
    above_near_ref,
    above_far_ref,
    west_ref,
    east_ref,
    center_ref,
):
    width = center_ref.shape[1]
    near, far = below_near_ref.shape[0], below_far_ref.shape[0]
    f32 = jnp.float32
    below = jnp.concatenate([below_near_ref[...].astype(f32), below_far_ref[...].astype(f32)])
    above = jnp.concatenate([above_far_ref[...].astype(f32), above_near_ref[...].astype(f32)])
    total = level_ref[...] + below + above
    west_ref[...] = total[:, :width].astype(jnp.bfloat16)
    center_ref[...] = total[:, width : 2 * width]
    east_ref[...] = total[:, 2 * width :].astype(jnp.bfloat16)


def row_sum(level, received):
    pixels, wide = level.shape
    side = like((pixels, wide // 3), jnp.bfloat16)
    return pl.pallas_call(
        row_sum_kernel,
        out_shape=(
            side,
            side,
            like((pixels, wide // 3), jnp.float32),
        ),
        in_specs=[VMEM] * 5,
        out_specs=(VMEM,) * 3,
        compiler_params=params(),
        cost_estimate=cost(3 * pixels * wide, 8 * pixels * wide),
    )(level, *received)


def head_kernel(
    place_ref,
    point_ref,
    center_ref,
    from_east_ref,
    from_west_ref,
    project_ref,
    upstream_ref,
    pixel_weight_ref,
    head_ref,
    grads_ref,
    message_ref,
    mine_ref,
    *terms_refs,
):
    bf16, f32 = jnp.bfloat16, jnp.float32
    width = point_ref.shape[1]
    xh = place_ref[2]
    pre_list = [
        point_ref[...],
        center_ref[...] + from_east_ref[...].astype(f32) + from_west_ref[...].astype(f32),
    ]
    gates = [sigmoid(pre) for pre in pre_list]
    acts = [(pre * gate).astype(bf16) for pre, gate in zip(pre_list, gates)]
    mixed = multiply(acts[0], project_ref[0]) + multiply(acts[1], project_ref[1])
    gate = sigmoid(mixed)
    head_ref[...] = (mixed * gate).astype(bf16)
    slope = gate * (1.0 + mixed * (1.0 - gate))
    out_grad = (upstream_ref[...].astype(f32) * pixel_weight_ref[...] * slope).astype(bf16)
    grads = [
        (
            multiply_transposed(out_grad, project_ref[k])
            * (gates[k] * (1.0 + pre_list[k] * (1.0 - gates[k])))
        ).astype(bf16)
        for k in range(2)
    ]
    pixels = grads_ref.shape[0]
    grads_ref[:, :width] = grads[1]
    grads_ref[:, width:] = grads[0]
    message_ref[:pixels, :width] = grads[1]
    message_ref[:pixels, width:] = grads[0]
    for k in range(2):
        terms = contract_row_axes(acts[k], out_grad)
        for half, terms_ref in enumerate(terms_refs):
            terms_ref[width * k : width * (k + 1), :] = terms[:, 128 * half : 128 * half + 128]
    count, part, _ = mine_ref.shape
    for y in range(count):
        rows = slice(pixels + y % 2 * part, pixels + y % 2 * part + part)
        for half, terms_ref in enumerate(terms_refs):
            even = terms_ref[pl.ds(2 * y, part, stride=2 * count), :]
            odd = terms_ref[pl.ds(2 * y + 1, part, stride=2 * count), :]
            lanes = slice(128 * half, 128 * half + 128)
            mine_ref[y, :, lanes] = jnp.where(xh == 0, even, odd)
            low = y // 2 * width + 128 * half
            message_ref[rows, low : low + 128] = jnp.where(xh == 0, odd, even).astype(bf16)


def head(place, point_pre, center, from_east, from_west, project, upstream, pixel_weight):
    pixels, width = point_pre.shape
    count = AXIS_SIZES["y"]
    part = width // count
    bf16, f32 = jnp.bfloat16, jnp.float32
    return pl.pallas_call(
        head_kernel,
        out_shape=(
            like((pixels, width), bf16),
            like((pixels, 2 * width), bf16),
            like((pixels + 2 * part, 2 * width), bf16),
            like((count, part, width), f32),
        ),
        in_specs=[SMEM] + [VMEM] * 7,
        out_specs=(VMEM,) * 4,
        scratch_shapes=[pltpu.VMEM((2 * width, 128), f32)] * (width // 128),
        compiler_params=params(),
        cost_estimate=cost(12 * pixels * width * width, 24 * pixels * width),
    )(place, point_pre, center, from_east, from_west, project, upstream, pixel_weight)


def forward_kernel(
    grads_ref,
    received_ref,
    mine_ref,
    after_east_ref,
    after_west_ref,
    features_in_ref,
    message_ref,
    features_out_ref,
):
    count, part, width = mine_ref.shape
    pixels = grads_ref.shape[0]
    for at in range(count):
        for slot, piece_ref in enumerate((grads_ref, received_ref)):
            for k in (0, 1):
                first = (2 * slot + k) * pixels
                message_ref[at, first : first + pixels, :] = piece_ref[
                    :pixels, k * width : (k + 1) * width
                ]
        rows = slice(pixels + at % 2 * part, pixels + at % 2 * part + part)
        low = at // 2 * width
        terms = mine_ref[at] + received_ref[rows, low : low + width].astype(jnp.float32)
        message_ref[at, 4 * pixels :, :] = terms.astype(jnp.bfloat16)


def forward(grads, received, mine, after, features):
    count, part, width = mine.shape
    pixels = grads.shape[0]
    return pl.pallas_call(
        forward_kernel,
        out_shape=(
            like((count, 4 * pixels + part, width), jnp.bfloat16),
            like(features.shape, features.dtype),
        ),
        in_specs=[VMEM] * 3 + [ANY] * 3,
        out_specs=(VMEM, ANY),
        input_output_aliases={5: 1},
        compiler_params=params(),
        cost_estimate=cost(mine.size, 8 * received.size),
    )(grads, received, mine, *after, features)


def weight_terms_kernel(
    span,
    chunk,
    place_ref,
    center_in_ref,
    east_first_ref,
    east_second_ref,
    west_first_ref,
    west_second_ref,
    message_in_ref,
    east_grad_ref,
    west_grad_ref,
    kept_ref,
    sent_ref,
    windows_ref,
    up_near_ref,
    up_far_ref,
    down_near_ref,
    down_far_ref,
    framed_ref,
    features_ref,
    message_ref,
    semaphores,
):
    _, total, width = features_ref.shape
    first_rows = east_first_ref.shape[0]
    message_copy = pltpu.make_async_copy(message_in_ref, message_ref, semaphores.at[0])
    copies = {
        0: [pltpu.make_async_copy(center_in_ref, features_ref.at[0], semaphores.at[1])],
        1: [
            pltpu.make_async_copy(
                east_first_ref, features_ref.at[1, pl.ds(0, first_rows)], semaphores.at[2]
            ),
            pltpu.make_async_copy(
                east_second_ref,
                features_ref.at[1, pl.ds(first_rows, total - first_rows)],
                semaphores.at[3],
            ),
        ],
        -1: [
            pltpu.make_async_copy(
                west_first_ref, features_ref.at[2, pl.ds(0, first_rows)], semaphores.at[4]
            ),
            pltpu.make_async_copy(
                west_second_ref,
                features_ref.at[2, pl.ds(first_rows, total - first_rows)],
                semaphores.at[5],
            ),
        ],
    }
    message_copy.start()
    for j in (0, 1, -1):
        for copy in copies[j]:
            copy.start()
    pixels = total // LAT_COUNT
    room = padded(chunk)
    core, y, xh = place_ref[0], place_ref[1], place_ref[2]
    far = up_far_ref.shape[0]

    edge = jnp.zeros((span, width), framed_ref.dtype)
    framed_ref[total : total + span, :width] = edge
    framed_ref[span : 2 * span, 2 * width : 3 * width] = edge
    message_copy.wait()
    for at in range(message_ref.shape[0]):
        for slot in (0, 1):
            band = 2 * at + (xh + slot) % 2
            low = 2 * slot * pixels
            piece = message_ref[at, low : low + pixels, :]
            for i in (-1, 0, 1):
                first = pl.multiple_of(span + span * i + band * pixels, 16)
                framed_ref[pl.ds(first, pixels), (i + 1) * width : (i + 2) * width] = piece
            first = pl.multiple_of(span + band * pixels, 16)
            framed_ref[pl.ds(first, pixels), 3 * width :] = message_ref[
                at, low + pixels : low + 2 * pixels, :
            ]
    for at, side_ref in enumerate((east_grad_ref, west_grad_ref)):
        lanes = slice(at * width, (at + 1) * width)
        side = side_ref[...]
        up_near_ref[:, lanes] = side[far:]
        up_far_ref[:, lanes] = side[:far]
        down_near_ref[:, lanes] = side[: pixels - far]
        down_far_ref[:, lanes] = side[pixels - far :]
    own_rows = pl.ds(pl.multiple_of(span + (2 * y + xh) * pixels, 16), pixels)
    windows_ref[...] = framed_ref[own_rows, : 3 * width]

    def store(first, value):
        count = value.shape[0]
        pieces = []
        at = 0
        while at < count:
            index, offset = divmod(first + at, chunk)
            size = min(chunk - offset, count - at)
            pieces.append((index, offset, at, size))
            at += size
        for owner in (0, 1):

            @pl.when(core == owner)
            def _():
                for index, offset, at, size in pieces:
                    target = kept_ref if index % 2 == owner else sent_ref
                    first_row = index // 2 * room + offset
                    target[first_row : first_row + size, :] = value[at : at + size]

    for j in (0, 1, -1):
        wide = 4 * width if j == 0 else 3 * width
        for copy in copies[j]:
            copy.wait()
        product = contract_row_axes(features_ref[j % 3], framed_ref[span : span + total, :wide])
        for i in (-1, 0, 1):
            store((3 * (i + 1) + j + 1) * width, product[:, (i + 1) * width : (i + 2) * width])
        if j == 0:
            project_rows = jnp.sum(message_ref[:, 4 * pixels :, :].astype(jnp.float32), axis=0)
            store(9 * width, project_rows)
            store(9 * width + project_rows.shape[0], product[:, 3 * width :])


def padded(chunk):
    return (chunk + 7) // 8 * 8


def weight_terms(span, place, features, message, sides):
    total, width = features[0].shape
    pixels = total // LAT_COUNT
    far = span % pixels
    chunk = (10 * width + message.shape[1] - 4 * pixels) // LON_COUNT
    out = like((LON_COUNT // 2 * padded(chunk), width), jnp.float32)
    near_shape = like((pixels - far, 2 * width), jnp.bfloat16)
    far_shape = like((far, 2 * width), jnp.bfloat16)
    return pl.pallas_call(
        functools.partial(weight_terms_kernel, span, chunk),
        out_shape=(out, out, like((pixels, 3 * width), jnp.bfloat16))
        + (near_shape, far_shape, near_shape, far_shape),
        in_specs=[SMEM] + [ANY] * 6 + [VMEM] * 2,
        out_specs=(VMEM,) * 7,
        scratch_shapes=[
            pltpu.VMEM((2 * span + total, 4 * width), jnp.bfloat16),
            pltpu.VMEM((3, total, width), jnp.bfloat16),
            pltpu.VMEM(message.shape, jnp.bfloat16),
            pltpu.SemaphoreType.DMA((6,)),
        ],
        compiler_params=params(60),
        cost_estimate=cost(20 * total * width * width, 8 * 2**20),
    )(place, *features, message, *sides)


def pair_sum_kernel(kept_ref, received_ref, out_ref):
    count, chunk, _ = out_ref.shape
    room = kept_ref.shape[0] // count
    for at in range(count):
        rows = slice(room * at, room * at + chunk)
        out_ref[at] = (kept_ref[rows, :] + received_ref[rows, :]).astype(jnp.bfloat16)


def pair_sum(kept, received, chunk):
    width = kept.shape[1]
    steps, count = 4, LON_COUNT // 2
    block = pl.BlockSpec((kept.shape[0] // steps, width), lambda s: (s, 0))
    return pl.pallas_call(
        pair_sum_kernel,
        grid=(steps,),
        out_shape=like((count, chunk, width), jnp.bfloat16),
        in_specs=[block, block],
        out_specs=pl.BlockSpec((count // steps, chunk, width), lambda s: (s, 0, 0)),
        compiler_params=params(),
        cost_estimate=cost(kept.size, 10 * kept.size),
    )(kept, received)


def piece_sum_kernel(pieces_ref, *refs):
    out_ref = refs[-1]
    total = pieces_ref[0].astype(jnp.float32)
    for at in range(1, pieces_ref.shape[0]):
        total = total + pieces_ref[at].astype(jnp.float32)
    for at in range(out_ref.shape[0]):
        out_ref[at] = total


def piece_sum(pieces, after):
    return pl.pallas_call(
        piece_sum_kernel,
        out_shape=like((LAT_COUNT,) + pieces.shape[1:], jnp.float32),
        in_specs=[VMEM] + [ANY] * len(after),
        out_specs=VMEM,
        compiler_params=params(),
        cost_estimate=cost(pieces.size, 4 * pieces.size),
    )(pieces, *after)


def interleave_kernel(parts_ref, out_ref, *sorted_refs):
    count, size, _ = parts_ref.shape
    for half, sorted_ref in enumerate(sorted_refs):
        lanes = slice(128 * half, 128 * half + 128)
        for a in range(count):
            sorted_ref[pl.ds(a, size, stride=count), :] = parts_ref[a, :, lanes]
        out_ref[:, lanes] = sorted_ref[...]


def interleave(parts):
    count, size, width = parts.shape
    return pl.pallas_call(
        interleave_kernel,
        out_shape=like((count * size, width), jnp.float32),
        in_specs=[VMEM],
        out_specs=VMEM,
        scratch_shapes=[pltpu.VMEM((count * size, 128), jnp.float32)] * (width // 128),
        compiler_params=params(),
        cost_estimate=cost(parts.size, 8 * parts.size),
    )(parts)


def add_product(total_ref, window, tap_ref, first):
    size = 512
    for low in range(0, total_ref.shape[1], size):
        lanes = slice(low, low + size)
        product = multiply_transposed(window, tap_ref[low : low + size, :])
        total_ref[:, lanes] = product if first else total_ref[:, lanes] + product


def input_gradient_kernel(
    windows_ref,
    grads_ref,
    east_ref,
    west_ref,
    up_near_ref,
    up_far_ref,
    down_near_ref,
    down_far_ref,
    kernel_ref,
    point_weight_ref,
    out_ref,
    total_ref,
    buffer_ref,
    semaphores,
    *row_refs,
):
    width = buffer_ref.shape[2]
    cols, rows, _ = out_ref.shape
    sources = [point_weight_ref] + [kernel_ref.at[tap] for tap in (1, 4, 7, 2, 5, 8, 0, 3, 6)]
    for at, tap_ref in enumerate(stream(sources, buffer_ref, semaphores)):
        side, i = divmod(at - 4, 3)
        lanes = slice(side * width, (side + 1) * width)
        if at == 0:
            window = grads_ref[:, width:]
        elif at < 4:
            window = windows_ref[:, (at - 1) * width : at * width]
        elif i == 0:
            window = jnp.concatenate([up_near_ref[:, lanes], up_far_ref[:, lanes]])
        elif i == 1:
            window = (east_ref, west_ref)[side][...]
        else:
            window = jnp.concatenate([down_far_ref[:, lanes], down_near_ref[:, lanes]])
        add_product(total_ref, window, tap_ref, at == 0)
    for block, row_ref in enumerate(row_refs):
        lanes = slice(128 * block, 128 * block + 128)
        row_ref[...] = total_ref[:, lanes]
        for col in range(cols):
            out_ref[col, :, lanes] = row_ref[pl.ds(col, rows, stride=cols), :].astype(out_ref.dtype)


def input_gradient(rows, windows, grads, east, west, side_rows, kernel, point_weight):
    pixels = grads.shape[0]
    in_width, width = point_weight.shape
    return pl.pallas_call(
        input_gradient_kernel,
        out_shape=like((pixels // rows, rows, in_width), jnp.bfloat16),
        in_specs=[VMEM] * 8 + [ANY] * 2,
        out_specs=VMEM,
        scratch_shapes=[pltpu.VMEM((pixels, in_width), jnp.float32)]
        + stream_scratch(in_width, width)
        + [pltpu.VMEM((pixels, 128), jnp.float32)] * (in_width // 128),
        compiler_params=params(60),
        cost_estimate=cost(20 * pixels * in_width * width, 40 * in_width * width),
    )(windows, grads, east, west, *side_rows, kernel, point_weight)


def shards(features, kernel, point_weight, project_weight, upstream, labels, class_weights):
    rows, cols, in_width = features.shape
    width = point_weight.shape[1]
    pixels = rows * cols
    place = jnp.stack([lax.axis_index("c"), lax.axis_index("y"), lax.axis_index("xh")])
    near = ATROUS_DILATION // rows
    far_pixels = (ATROUS_DILATION - near * rows) * cols
    tiles_over = ATROUS_DILATION // cols
    span = ATROUS_DILATION * cols

    flat, slices = channel_slices(features)
    below_near, below_far, above_near, above_far, level, point_pre = tap_products(
        flat, kernel, point_weight, far_pixels, slices
    )
    received = (
        shift_rows(below_near, -near),
        shift_rows(below_far, -(near + 1)),
        shift_rows(above_near, near),
        shift_rows(above_far, near + 1),
    )
    column_features = lax.all_to_all(slices, LAT, 0, 0).reshape(LAT_COUNT * pixels, -1)
    first_rows = FIRST_BANDS * pixels
    first_features, second_features = column_features[:first_rows], column_features[first_rows:]
    to_east, to_west, center = row_sum(level, received)
    from_east = shift_columns(to_west, -tiles_over)
    from_west = shift_columns(to_east, tiles_over)
    class_index = jnp.arange(3, dtype=jnp.int32)
    pixel_weight = jnp.sum(
        jnp.where(labels[..., None] == class_index, class_weights, 0.0), axis=-1
    ).reshape(-1, 1)
    head_out, grads, message, mine = head(
        place,
        point_pre,
        center,
        from_east,
        from_west,
        project_weight,
        upstream.reshape(pixels, width),
        pixel_weight,
    )

    other = lax.ppermute(message, "xh", [(0, 1), (1, 0)])
    first_east = shift_columns(first_features, -tiles_over)
    first_west = shift_columns(first_features, tiles_over)
    message, second_features = forward(
        grads, other, mine, (first_east, first_west), second_features
    )
    gathered = lax.all_to_all(message, "y", 0, 0)
    second_east = shift_columns(second_features, -tiles_over)
    second_west = shift_columns(second_features, tiles_over)
    east_grad = shift_columns(grads[:, :width], tiles_over)
    west_grad = shift_columns(grads[:, :width], -tiles_over)

    kept, sent, windows, up_near, up_far, down_near, down_far = weight_terms(
        span,
        place,
        (column_features, first_east, second_east, first_west, second_west),
        gathered,
        (east_grad, west_grad),
    )
    side_rows = (
        shift_rows(up_near, -near),
        shift_rows(up_far, -(near + 1)),
        shift_rows(down_near, near),
        shift_rows(down_far, near + 1),
    )
    chunk = (10 * in_width + 2 * width) // (LAT_COUNT * LON_COUNT)
    chip_sum = pair_sum(kept, lax.ppermute(sent, "c", [(0, 1), (1, 0)]), chunk)
    pieces = lax.all_to_all(chip_sum, ("xl", "z"), 0, 0)

    weight_grads = interleave(lax.all_to_all(piece_sum(pieces, side_rows), LAT, 0, 0))
    input_grad = input_gradient(
        rows, windows, grads, east_grad, west_grad, side_rows, kernel, point_weight
    )

    head_tile = head_out.reshape(rows, cols, width)
    grad_tile = jnp.swapaxes(input_grad, 0, 1)
    return (head_tile, grad_tile, weight_grads)


def solution(mesh):
    split = Mesh(mesh.devices.reshape(tuple(AXIS_SIZES.values())), tuple(AXIS_SIZES))
    tile = P(LAT, LON, None)
    return jax.shard_map(
        shards,
        mesh=split,
        in_specs=(tile, P(), P(), P(), tile, P(LAT, LON), P()),
        out_specs=(tile, tile, P(LON, None)),
        check_vma=False,
    )
```

```python
import functools

import jax
import jax.numpy as jnp
from jax import lax
from jax.experimental import pallas as pl
from jax.experimental.pallas import tpu as pltpu
from jax.sharding import Mesh, PartitionSpec as P

ATROUS_DILATION = 36
LAT = ("y", "xh")
LON = ("xl", "z", "c")
AXIS_SIZES = {"y": 4, "xh": 2, "xl": 2, "z": 8, "c": 2}
LAT_COUNT = 8
LON_COUNT = 32
FIRST_BANDS = 4
VMEM = pl.BlockSpec(memory_space=pltpu.VMEM)
SMEM = pl.BlockSpec(memory_space=pltpu.SMEM)
ANY = pl.BlockSpec(memory_space=pl.ANY)


def shift_rows(value, by):
    pairs = [(i, i + by) for i in range(LAT_COUNT) if 0 <= i + by < LAT_COUNT]
    return lax.ppermute(value, LAT, pairs)


def shift_columns(value, by):
    return lax.ppermute(value, LON, [(i, (i + by) % LON_COUNT) for i in range(LON_COUNT)])


def contract_row_axes(left, right):
    return lax.dot_general(
        left, right, (((0,), (0,)), ((), ())), preferred_element_type=jnp.float32
    )


def multiply_transposed(left, right):
    return lax.dot_general(
        left, right, (((1,), (1,)), ((), ())), preferred_element_type=jnp.float32
    )


def multiply(left, right):
    return jnp.dot(left, right, preferred_element_type=jnp.float32)


def sigmoid(value):
    return 1.0 / (1.0 + jnp.exp(-value))


def params(megabytes=24):
    return pltpu.CompilerParams(vmem_limit_bytes=megabytes * 2**20)


def cost(flops, moved):
    return pl.CostEstimate(flops=int(flops), bytes_accessed=int(moved), transcendentals=0)


def like(shape, dtype):
    return jax.ShapeDtypeStruct(shape, dtype)


def stream(sources, buffer_ref, semaphores):
    depth = buffer_ref.shape[0]

    def copy(at):
        return pltpu.make_async_copy(
            sources[at], buffer_ref.at[at % depth], semaphores.at[at % depth]
        )

    for at in range(min(depth - 1, len(sources))):
        copy(at).start()
    for at in range(len(sources)):
        if at + depth - 1 < len(sources):
            copy(at + depth - 1).start()
        copy(at).wait()
        yield buffer_ref.at[at % depth]


STREAM_DEPTH = 6


def stream_scratch(in_width, width):
    return [
        pltpu.VMEM((STREAM_DEPTH, in_width, width), jnp.bfloat16),
        pltpu.SemaphoreType.DMA((STREAM_DEPTH,)),
    ]


def products_kernel(
    flat_ref,
    kernel_ref,
    point_weight_ref,
    after_ref,
    below_near_ref,
    below_far_ref,
    above_near_ref,
    above_far_ref,
    level_ref,
    point_ref,
):
    width = kernel_ref.shape[2]
    pixels = flat_ref.shape[0]
    far = below_far_ref.shape[0]
    for at, tap in enumerate((6, 7, 8, 0, 1, 2, 3, 4, 5)):
        product = multiply(flat_ref[...], kernel_ref[tap])
        rounded = product.astype(jnp.bfloat16)
        lanes = slice((at % 3) * width, (at % 3 + 1) * width)
        if at < 3:
            below_far_ref[:, lanes] = rounded[:far]
            below_near_ref[:, lanes] = rounded[far:]
        elif at < 6:
            above_near_ref[:, lanes] = rounded[: pixels - far]
            above_far_ref[:, lanes] = rounded[pixels - far :]
        else:
            level_ref[:, lanes] = product
    point_ref[...] = multiply(flat_ref[...], point_weight_ref[...])


def tap_products(flat, kernel, point_weight, far, after):
    pixels, in_width = flat.shape
    width = kernel.shape[2]
    near_shape = like((pixels - far, 3 * width), jnp.bfloat16)
    far_shape = like((far, 3 * width), jnp.bfloat16)
    return pl.pallas_call(
        products_kernel,
        out_shape=(near_shape, far_shape, near_shape, far_shape)
        + (like((pixels, 3 * width), jnp.float32), like((pixels, width), jnp.float32)),
        in_specs=[VMEM] * 3 + [ANY],
        out_specs=(VMEM,) * 6,
        compiler_params=params(),
        cost_estimate=cost(20 * pixels * in_width * width, 20 * in_width * width),
    )(flat, kernel, point_weight, after)


def slices_kernel(columns_ref, flat_ref, slices_ref, *row_refs):
    cols, rows, _ = columns_ref.shape
    for block, row_ref in enumerate(row_refs):
        lanes = slice(128 * block, 128 * block + 128)
        for col in range(cols):
            row_ref[pl.ds(col, rows, stride=cols), :] = columns_ref[col, :, lanes].astype(
                jnp.float32
            )
        flat_ref[:, lanes] = row_ref[...].astype(jnp.bfloat16)
    count, _, size = slices_ref.shape
    part = size // count
    source = lax.broadcasted_iota(jnp.int32, (size, size), 0)
    target = lax.broadcasted_iota(jnp.int32, (size, size), 1)
    wanted = (source % count) * part + source // count
    picker = jnp.where(target == wanted, 1.0, 0.0).astype(jnp.bfloat16)
    sorted_blocks = [
        multiply(flat_ref[:, size * b : size * (b + 1)], picker).astype(jnp.bfloat16)
        for b in range(count)
    ]
    for a in range(count):
        slices_ref[a] = jnp.concatenate(
            [block[:, part * a : part * (a + 1)] for block in sorted_blocks], axis=1
        )


def channel_slices(features):
    rows, cols, in_width = features.shape
    pixels = rows * cols
    return pl.pallas_call(
        slices_kernel,
        out_shape=(
            like((pixels, in_width), jnp.bfloat16),
            like((LAT_COUNT, pixels, in_width // LAT_COUNT), jnp.bfloat16),
        ),
        in_specs=[VMEM],
        out_specs=(VMEM,) * 2,
        scratch_shapes=[pltpu.VMEM((pixels, 128), jnp.float32)] * (in_width // 128),
        compiler_params=params(),
        cost_estimate=cost(2 * pixels * in_width * in_width // LAT_COUNT, 6 * pixels * in_width),
    )(jnp.swapaxes(features, 0, 1))


def row_sum_kernel(
    level_ref,
    below_near_ref,
    below_far_ref,
    above_near_ref,
    above_far_ref,
    west_ref,
    east_ref,
    center_ref,
):
    width = center_ref.shape[1]
    near, far = below_near_ref.shape[0], below_far_ref.shape[0]
    f32 = jnp.float32
    below = jnp.concatenate([below_near_ref[...].astype(f32), below_far_ref[...].astype(f32)])
    above = jnp.concatenate([above_far_ref[...].astype(f32), above_near_ref[...].astype(f32)])
    total = level_ref[...] + below + above
    west_ref[...] = total[:, :width].astype(jnp.bfloat16)
    center_ref[...] = total[:, width : 2 * width]
    east_ref[...] = total[:, 2 * width :].astype(jnp.bfloat16)


def row_sum(level, received):
    pixels, wide = level.shape
    side = like((pixels, wide // 3), jnp.bfloat16)
    return pl.pallas_call(
        row_sum_kernel,
        out_shape=(
            side,
            side,
            like((pixels, wide // 3), jnp.float32),
        ),
        in_specs=[VMEM] * 5,
        out_specs=(VMEM,) * 3,
        compiler_params=params(),
        cost_estimate=cost(3 * pixels * wide, 8 * pixels * wide),
    )(level, *received)


def head_kernel(
    place_ref,
    point_ref,
    center_ref,
    from_east_ref,
    from_west_ref,
    project_ref,
    upstream_ref,
    pixel_weight_ref,
    head_ref,
    grads_ref,
    message_ref,
    mine_ref,
    *terms_refs,
):
    bf16, f32 = jnp.bfloat16, jnp.float32
    width = point_ref.shape[1]
    xh = place_ref[2]
    pre_list = [
        point_ref[...],
        center_ref[...] + from_east_ref[...].astype(f32) + from_west_ref[...].astype(f32),
    ]
    gates = [sigmoid(pre) for pre in pre_list]
    acts = [(pre * gate).astype(bf16) for pre, gate in zip(pre_list, gates)]
    mixed = multiply(acts[0], project_ref[0]) + multiply(acts[1], project_ref[1])
    gate = sigmoid(mixed)
    out = mixed * gate
    cols, rows, _ = head_ref.shape
    for half, row_ref in enumerate(terms_refs):
        lanes = slice(128 * half, 128 * half + 128)
        row_ref[: cols * rows, :] = out[:, lanes]
        for col in range(cols):
            head_ref[col, :, lanes] = row_ref[pl.ds(col, rows, stride=cols), :].astype(bf16)
    slope = gate * (1.0 + mixed * (1.0 - gate))
    out_grad = (upstream_ref[...].astype(f32) * pixel_weight_ref[...] * slope).astype(bf16)
    grads = [
        (
            multiply_transposed(out_grad, project_ref[k])
            * (gates[k] * (1.0 + pre_list[k] * (1.0 - gates[k])))
        ).astype(bf16)
        for k in range(2)
    ]
    pixels = grads_ref.shape[0]
    grads_ref[:, :width] = grads[1]
    grads_ref[:, width:] = grads[0]
    message_ref[:pixels, :width] = grads[1]
    message_ref[:pixels, width:] = grads[0]
    for k in range(2):
        terms = contract_row_axes(acts[k], out_grad)
        for half, terms_ref in enumerate(terms_refs):
            terms_ref[width * k : width * (k + 1), :] = terms[:, 128 * half : 128 * half + 128]
    count, part, _ = mine_ref.shape
    for y in range(count):
        rows = slice(pixels + y % 2 * part, pixels + y % 2 * part + part)
        for half, terms_ref in enumerate(terms_refs):
            even = terms_ref[pl.ds(2 * y, part, stride=2 * count), :]
            odd = terms_ref[pl.ds(2 * y + 1, part, stride=2 * count), :]
            lanes = slice(128 * half, 128 * half + 128)
            mine_ref[y, :, lanes] = jnp.where(xh == 0, even, odd)
            low = y // 2 * width + 128 * half
            message_ref[rows, low : low + 128] = jnp.where(xh == 0, odd, even).astype(bf16)


def head(
    rows, place, point_pre, center, from_east, from_west, project, upstream, pixel_weight
):
    pixels, width = point_pre.shape
    count = AXIS_SIZES["y"]
    part = width // count
    bf16, f32 = jnp.bfloat16, jnp.float32
    return pl.pallas_call(
        head_kernel,
        out_shape=(
            like((pixels // rows, rows, width), bf16),
            like((pixels, 2 * width), bf16),
            like((pixels + 2 * part, 2 * width), bf16),
            like((count, part, width), f32),
        ),
        in_specs=[SMEM] + [VMEM] * 7,
        out_specs=(VMEM,) * 4,
        scratch_shapes=[pltpu.VMEM((2 * width, 128), f32)] * (width // 128),
        compiler_params=params(),
        cost_estimate=cost(12 * pixels * width * width, 24 * pixels * width),
    )(place, point_pre, center, from_east, from_west, project, upstream, pixel_weight)


def forward_kernel(
    grads_ref,
    received_ref,
    mine_ref,
    after_east_ref,
    after_west_ref,
    features_in_ref,
    message_ref,
    features_out_ref,
):
    count, part, width = mine_ref.shape
    pixels = grads_ref.shape[0]
    for at in range(count):
        for slot, piece_ref in enumerate((grads_ref, received_ref)):
            for k in (0, 1):
                first = (2 * slot + k) * pixels
                message_ref[at, first : first + pixels, :] = piece_ref[
                    :pixels, k * width : (k + 1) * width
                ]
        rows = slice(pixels + at % 2 * part, pixels + at % 2 * part + part)
        low = at // 2 * width
        terms = mine_ref[at] + received_ref[rows, low : low + width].astype(jnp.float32)
        message_ref[at, 4 * pixels :, :] = terms.astype(jnp.bfloat16)


def forward(grads, received, mine, after, features):
    count, part, width = mine.shape
    pixels = grads.shape[0]
    return pl.pallas_call(
        forward_kernel,
        out_shape=(
            like((count, 4 * pixels + part, width), jnp.bfloat16),
            like(features.shape, features.dtype),
        ),
        in_specs=[VMEM] * 3 + [ANY] * 3,
        out_specs=(VMEM, ANY),
        input_output_aliases={5: 1},
        compiler_params=params(),
        cost_estimate=cost(mine.size, 8 * received.size),
    )(grads, received, mine, *after, features)


def weight_terms_kernel(
    span,
    chunk,
    place_ref,
    center_in_ref,
    east_first_ref,
    east_second_ref,
    west_first_ref,
    west_second_ref,
    message_in_ref,
    after_east_ref,
    after_west_ref,
    kept_ref,
    rounded_ref,
    windows_ref,
    framed_ref,
    features_ref,
    message_ref,
    sent_ref,
    semaphores,
):
    _, total, width = features_ref.shape
    first_rows = east_first_ref.shape[0]
    message_copy = pltpu.make_async_copy(message_in_ref, message_ref, semaphores.at[0])
    copies = {
        0: [pltpu.make_async_copy(center_in_ref, features_ref.at[0], semaphores.at[1])],
        1: [
            pltpu.make_async_copy(
                east_first_ref, features_ref.at[1, pl.ds(0, first_rows)], semaphores.at[2]
            ),
            pltpu.make_async_copy(
                east_second_ref,
                features_ref.at[1, pl.ds(first_rows, total - first_rows)],
                semaphores.at[3],
            ),
        ],
        -1: [
            pltpu.make_async_copy(
                west_first_ref, features_ref.at[2, pl.ds(0, first_rows)], semaphores.at[4]
            ),
            pltpu.make_async_copy(
                west_second_ref,
                features_ref.at[2, pl.ds(first_rows, total - first_rows)],
                semaphores.at[5],
            ),
        ],
    }
    message_copy.start()
    for j in (0, 1, -1):
        for copy in copies[j]:
            copy.start()
    pixels = total // LAT_COUNT
    room = padded(chunk)
    core, y, xh = place_ref[0], place_ref[1], place_ref[2]

    edge = jnp.zeros((span, width), framed_ref.dtype)
    framed_ref[total : total + span, :width] = edge
    framed_ref[span : 2 * span, 2 * width : 3 * width] = edge
    message_copy.wait()
    for at in range(message_ref.shape[0]):
        for slot in (0, 1):
            band = 2 * at + (xh + slot) % 2
            low = 2 * slot * pixels
            piece = message_ref[at, low : low + pixels, :]
            for i in (-1, 0, 1):
                first = pl.multiple_of(span + span * i + band * pixels, 16)
                framed_ref[pl.ds(first, pixels), (i + 1) * width : (i + 2) * width] = piece
            first = pl.multiple_of(span + band * pixels, 16)
            framed_ref[pl.ds(first, pixels), 3 * width :] = message_ref[
                at, low + pixels : low + 2 * pixels, :
            ]
    own_rows = pl.ds(pl.multiple_of(span + (2 * y + xh) * pixels, 16), pixels)
    windows_ref[...] = framed_ref[own_rows, : 3 * width]

    def store(first, value):
        count = value.shape[0]
        pieces = []
        at = 0
        while at < count:
            index, offset = divmod(first + at, chunk)
            size = min(chunk - offset, count - at)
            pieces.append((index, offset, at, size))
            at += size
        for owner in (0, 1):

            @pl.when(core == owner)
            def _():
                for index, offset, at, size in pieces:
                    target = kept_ref if index % 2 == owner else sent_ref
                    first_row = index // 2 * room + offset
                    target[first_row : first_row + size, :] = value[at : at + size]

    for j in (0, 1, -1):
        wide = 4 * width if j == 0 else 3 * width
        for copy in copies[j]:
            copy.wait()
        product = contract_row_axes(features_ref[j % 3], framed_ref[span : span + total, :wide])
        for i in (-1, 0, 1):
            store((3 * (i + 1) + j + 1) * width, product[:, (i + 1) * width : (i + 2) * width])
        if j == 0:
            project_rows = jnp.sum(message_ref[:, 4 * pixels :, :].astype(jnp.float32), axis=0)
            store(9 * width, project_rows)
            store(9 * width + project_rows.shape[0], product[:, 3 * width :])
    rounded_ref[...] = sent_ref[...].astype(rounded_ref.dtype)


def padded(chunk):
    return (chunk + 15) // 16 * 16


def weight_terms(span, place, features, message, after):
    total, width = features[0].shape
    pixels = total // LAT_COUNT
    chunk = (10 * width + message.shape[1] - 4 * pixels) // LON_COUNT
    terms_shape = (LON_COUNT // 2 * padded(chunk), width)
    return pl.pallas_call(
        functools.partial(weight_terms_kernel, span, chunk),
        out_shape=(
            like(terms_shape, jnp.float32),
            like(terms_shape, jnp.bfloat16),
            like((pixels, 3 * width), jnp.bfloat16),
        ),
        in_specs=[SMEM] + [ANY] * 8,
        out_specs=(VMEM,) * 3,
        scratch_shapes=[
            pltpu.VMEM((2 * span + total, 4 * width), jnp.bfloat16),
            pltpu.VMEM((3, total, width), jnp.bfloat16),
            pltpu.VMEM(message.shape, jnp.bfloat16),
            pltpu.VMEM(terms_shape, jnp.float32),
            pltpu.SemaphoreType.DMA((6,)),
        ],
        compiler_params=params(60),
        cost_estimate=cost(20 * total * width * width, 8 * 2**20),
    )(place, *features, message, *after)


def pair_sum_kernel(kept_ref, received_ref, out_ref):
    count, chunk, _ = out_ref.shape
    room = kept_ref.shape[0] // count
    for at in range(count):
        rows = slice(room * at, room * (at + 1))
        total = kept_ref[rows, :] + received_ref[rows, :].astype(jnp.float32)
        out_ref[at] = total[:chunk].astype(jnp.bfloat16)


def pair_sum(kept, received, chunk):
    return pl.pallas_call(
        pair_sum_kernel,
        out_shape=like((LON_COUNT // 2, chunk, kept.shape[1]), jnp.bfloat16),
        in_specs=[VMEM] * 2,
        out_specs=VMEM,
        compiler_params=params(),
        cost_estimate=cost(kept.size, 10 * kept.size),
    )(kept, received)


def side_slices_kernel(
    east_grad_ref, west_grad_ref, up_near_ref, up_far_ref, down_near_ref, down_far_ref
):
    far = up_far_ref.shape[0]
    for at, side_ref in enumerate((east_grad_ref, west_grad_ref)):
        side = side_ref[...]
        pixels, width = side.shape
        lanes = slice(at * width, (at + 1) * width)
        up_near_ref[:, lanes] = side[far:]
        up_far_ref[:, lanes] = side[:far]
        down_near_ref[:, lanes] = side[: pixels - far]
        down_far_ref[:, lanes] = side[pixels - far :]


def side_slices(east_grad, west_grad, far):
    pixels, width = east_grad.shape
    near_shape = like((pixels - far, 2 * width), jnp.bfloat16)
    far_shape = like((far, 2 * width), jnp.bfloat16)
    return pl.pallas_call(
        side_slices_kernel,
        out_shape=(near_shape, far_shape, near_shape, far_shape),
        in_specs=[VMEM] * 2,
        out_specs=(VMEM,) * 4,
        compiler_params=params(),
        cost_estimate=cost(pixels * width, 8 * pixels * width),
    )(east_grad, west_grad)


def piece_sum_kernel(pieces_ref, *refs):
    out_ref = refs[-1]
    total = pieces_ref[0].astype(jnp.float32)
    for at in range(1, pieces_ref.shape[0]):
        total = total + pieces_ref[at].astype(jnp.float32)
    rounded = total.astype(out_ref.dtype)
    for at in range(out_ref.shape[0]):
        out_ref[at] = rounded


def piece_sum(pieces, after):
    return pl.pallas_call(
        piece_sum_kernel,
        out_shape=like((LAT_COUNT,) + pieces.shape[1:], jnp.bfloat16),
        in_specs=[VMEM] + [ANY] * len(after),
        out_specs=VMEM,
        compiler_params=params(),
        cost_estimate=cost(pieces.size, 4 * pieces.size),
    )(pieces, *after)


def interleave_kernel(parts_ref, out_ref, *sorted_refs):
    count, size, _ = parts_ref.shape
    for half, sorted_ref in enumerate(sorted_refs):
        lanes = slice(128 * half, 128 * half + 128)
        for a in range(count):
            sorted_ref[pl.ds(a, size, stride=count), :] = parts_ref[a, :, lanes].astype(
                jnp.float32
            )
        out_ref[:, lanes] = sorted_ref[...]


def interleave(parts):
    count, size, width = parts.shape
    return pl.pallas_call(
        interleave_kernel,
        out_shape=like((count * size, width), jnp.float32),
        in_specs=[VMEM],
        out_specs=VMEM,
        scratch_shapes=[pltpu.VMEM((count * size, 128), jnp.float32)] * (width // 128),
        compiler_params=params(),
        cost_estimate=cost(parts.size, 8 * parts.size),
    )(parts)


def add_product(total_ref, window, tap_ref, first):
    size = 512
    for low in range(0, total_ref.shape[1], size):
        lanes = slice(low, low + size)
        product = multiply_transposed(window, tap_ref[low : low + size, :])
        total_ref[:, lanes] = product if first else total_ref[:, lanes] + product


def input_gradient_kernel(
    windows_ref,
    grads_ref,
    east_ref,
    west_ref,
    up_near_ref,
    up_far_ref,
    down_near_ref,
    down_far_ref,
    kernel_ref,
    point_weight_ref,
    out_ref,
    total_ref,
    buffer_ref,
    semaphores,
    *row_refs,
):
    width = buffer_ref.shape[2]
    cols, rows, _ = out_ref.shape
    sources = [point_weight_ref] + [kernel_ref.at[tap] for tap in (1, 4, 7, 2, 5, 8, 0, 3, 6)]
    for at, tap_ref in enumerate(stream(sources, buffer_ref, semaphores)):
        side, i = divmod(at - 4, 3)
        lanes = slice(side * width, (side + 1) * width)
        if at == 0:
            window = grads_ref[:, width:]
        elif at < 4:
            window = windows_ref[:, (at - 1) * width : at * width]
        elif i == 0:
            window = jnp.concatenate([up_near_ref[:, lanes], up_far_ref[:, lanes]])
        elif i == 1:
            window = (east_ref, west_ref)[side][...]
        else:
            window = jnp.concatenate([down_far_ref[:, lanes], down_near_ref[:, lanes]])
        add_product(total_ref, window, tap_ref, at == 0)
    for block, row_ref in enumerate(row_refs):
        lanes = slice(128 * block, 128 * block + 128)
        row_ref[...] = total_ref[:, lanes]
        for col in range(cols):
            out_ref[col, :, lanes] = row_ref[pl.ds(col, rows, stride=cols), :].astype(out_ref.dtype)


def input_gradient(rows, windows, grads, east, west, side_rows, kernel, point_weight):
    pixels = grads.shape[0]
    in_width, width = point_weight.shape
    return pl.pallas_call(
        input_gradient_kernel,
        out_shape=like((pixels // rows, rows, in_width), jnp.bfloat16),
        in_specs=[VMEM] * 8 + [ANY] * 2,
        out_specs=VMEM,
        scratch_shapes=[pltpu.VMEM((pixels, in_width), jnp.float32)]
        + stream_scratch(in_width, width)
        + [pltpu.VMEM((pixels, 128), jnp.float32)] * (in_width // 128),
        compiler_params=params(60),
        cost_estimate=cost(20 * pixels * in_width * width, 40 * in_width * width),
    )(windows, grads, east, west, *side_rows, kernel, point_weight)


def shards(features, kernel, point_weight, project_weight, upstream, labels, class_weights):
    rows, cols, in_width = features.shape
    width = point_weight.shape[1]
    pixels = rows * cols
    place = jnp.stack([lax.axis_index("c"), lax.axis_index("y"), lax.axis_index("xh")])
    near = ATROUS_DILATION // rows
    far_pixels = (ATROUS_DILATION - near * rows) * cols
    tiles_over = ATROUS_DILATION // cols
    span = ATROUS_DILATION * cols

    flat, slices = channel_slices(features)
    below_near, below_far, above_near, above_far, level, point_pre = tap_products(
        flat, kernel, point_weight, far_pixels, slices
    )
    received = (
        shift_rows(below_near, -near),
        shift_rows(below_far, -(near + 1)),
        shift_rows(above_near, near),
        shift_rows(above_far, near + 1),
    )
    column_features = lax.all_to_all(slices, LAT, 0, 0).reshape(LAT_COUNT * pixels, -1)
    first_rows = FIRST_BANDS * pixels
    first_features, second_features = column_features[:first_rows], column_features[first_rows:]
    to_east, to_west, center = row_sum(level, received)
    from_east = shift_columns(to_west, -tiles_over)
    from_west = shift_columns(to_east, tiles_over)
    class_index = jnp.arange(3, dtype=jnp.int32)
    pixel_weight = jnp.sum(
        jnp.where(labels[..., None] == class_index, class_weights, 0.0), axis=-1
    ).reshape(-1, 1)
    head_out, grads, message, mine = head(
        rows,
        place,
        point_pre,
        center,
        from_east,
        from_west,
        project_weight,
        upstream.reshape(pixels, width),
        pixel_weight,
    )

    other = lax.ppermute(message, "xh", [(0, 1), (1, 0)])
    first_east = shift_columns(first_features, -tiles_over)
    first_west = shift_columns(first_features, tiles_over)
    message, second_features = forward(
        grads, other, mine, (first_east, first_west), second_features
    )
    gathered = lax.all_to_all(message, "y", 0, 0)
    second_east = shift_columns(second_features, -tiles_over)
    second_west = shift_columns(second_features, tiles_over)
    east_grad = shift_columns(grads[:, :width], tiles_over)
    west_grad = shift_columns(grads[:, :width], -tiles_over)

    kept, sent, windows = weight_terms(
        span,
        place,
        (column_features, first_east, second_east, first_west, second_west),
        gathered,
        (east_grad, west_grad),
    )
    chunk = (10 * in_width + 2 * width) // (LAT_COUNT * LON_COUNT)
    chip_sum = pair_sum(kept, lax.ppermute(sent, "c", [(0, 1), (1, 0)]), chunk)
    up_near, up_far, down_near, down_far = side_slices(east_grad, west_grad, far_pixels)
    side_rows = (
        shift_rows(up_near, -near),
        shift_rows(up_far, -(near + 1)),
        shift_rows(down_near, near),
        shift_rows(down_far, near + 1),
    )
    pieces = lax.all_to_all(chip_sum, ("xl", "z"), 0, 0)

    weight_grads = interleave(lax.all_to_all(piece_sum(pieces, side_rows), LAT, 0, 0))
    input_grad = input_gradient(
        rows, windows, grads, east_grad, west_grad, side_rows, kernel, point_weight
    )

    head_tile = jnp.swapaxes(head_out, 0, 1)
    grad_tile = jnp.swapaxes(input_grad, 0, 1)
    return (head_tile, grad_tile, weight_grads)


def solution(mesh):
    split = Mesh(mesh.devices.reshape(tuple(AXIS_SIZES.values())), tuple(AXIS_SIZES))
    tile = P(LAT, LON, None)
    return jax.shard_map(
        shards,
        mesh=split,
        in_specs=(tile, P(), P(), P(), tile, P(LAT, LON), P()),
        out_specs=(tile, tile, P(LON, None)),
        check_vma=False,
    )
```

```python
import functools

import jax
import jax.numpy as jnp
from jax import lax
from jax.experimental import pallas as pl
from jax.experimental.pallas import tpu as pltpu
from jax.sharding import Mesh, PartitionSpec as P

ATROUS_DILATION = 36
LAT = ("y", "xh")
LON = ("xl", "z", "c")
AXIS_SIZES = {"y": 4, "xh": 2, "xl": 2, "z": 8, "c": 2}
LAT_COUNT = 8
LON_COUNT = 32
FIRST_BANDS = 4
VMEM = pl.BlockSpec(memory_space=pltpu.VMEM)
SMEM = pl.BlockSpec(memory_space=pltpu.SMEM)
ANY = pl.BlockSpec(memory_space=pl.ANY)


def shift_rows(value, by):
    pairs = [(i, i + by) for i in range(LAT_COUNT) if 0 <= i + by < LAT_COUNT]
    return lax.ppermute(value, LAT, pairs)


def shift_columns(value, by):
    return lax.ppermute(value, LON, [(i, (i + by) % LON_COUNT) for i in range(LON_COUNT)])


def contract_row_axes(left, right):
    return lax.dot_general(
        left, right, (((0,), (0,)), ((), ())), preferred_element_type=jnp.float32
    )


def multiply_transposed(left, right):
    return lax.dot_general(
        left, right, (((1,), (1,)), ((), ())), preferred_element_type=jnp.float32
    )


def multiply(left, right):
    return jnp.dot(left, right, preferred_element_type=jnp.float32)


def sigmoid(value):
    return 1.0 / (1.0 + jnp.exp(-value))


def params(megabytes=24):
    return pltpu.CompilerParams(vmem_limit_bytes=megabytes * 2**20)


def cost(flops, moved):
    return pl.CostEstimate(flops=int(flops), bytes_accessed=int(moved), transcendentals=0)


def like(shape, dtype):
    return jax.ShapeDtypeStruct(shape, dtype)


def stream(sources, buffer_ref, semaphores):
    depth = buffer_ref.shape[0]

    def copy(at):
        return pltpu.make_async_copy(
            sources[at], buffer_ref.at[at % depth], semaphores.at[at % depth]
        )

    for at in range(min(depth - 1, len(sources))):
        copy(at).start()
    for at in range(len(sources)):
        if at + depth - 1 < len(sources):
            copy(at + depth - 1).start()
        copy(at).wait()
        yield buffer_ref.at[at % depth]


STREAM_DEPTH = 6


def stream_scratch(in_width, width):
    return [
        pltpu.VMEM((STREAM_DEPTH, in_width, width), jnp.bfloat16),
        pltpu.SemaphoreType.DMA((STREAM_DEPTH,)),
    ]


def products_kernel(
    flat_ref,
    kernel_ref,
    point_weight_ref,
    after_ref,
    below_near_ref,
    below_far_ref,
    above_near_ref,
    above_far_ref,
    level_ref,
    point_ref,
):
    width = kernel_ref.shape[2]
    pixels = flat_ref.shape[0]
    far = below_far_ref.shape[0]
    for at, tap in enumerate((6, 7, 8, 0, 1, 2, 3, 4, 5)):
        product = multiply(flat_ref[...], kernel_ref[tap])
        rounded = product.astype(jnp.bfloat16)
        lanes = slice((at % 3) * width, (at % 3 + 1) * width)
        if at < 3:
            below_far_ref[:, lanes] = rounded[:far]
            below_near_ref[:, lanes] = rounded[far:]
        elif at < 6:
            above_near_ref[:, lanes] = rounded[: pixels - far]
            above_far_ref[:, lanes] = rounded[pixels - far :]
        else:
            level_ref[:, lanes] = product
    point_ref[...] = multiply(flat_ref[...], point_weight_ref[...])


def tap_products(flat, kernel, point_weight, far, after):
    pixels, in_width = flat.shape
    width = kernel.shape[2]
    near_shape = like((pixels - far, 3 * width), jnp.bfloat16)
    far_shape = like((far, 3 * width), jnp.bfloat16)
    return pl.pallas_call(
        products_kernel,
        out_shape=(near_shape, far_shape, near_shape, far_shape)
        + (like((pixels, 3 * width), jnp.float32), like((pixels, width), jnp.float32)),
        in_specs=[VMEM] * 3 + [ANY],
        out_specs=(VMEM,) * 6,
        compiler_params=params(),
        cost_estimate=cost(20 * pixels * in_width * width, 20 * in_width * width),
    )(flat, kernel, point_weight, after)


def slices_kernel(columns_ref, flat_ref, slices_ref, *row_refs):
    cols, rows, _ = columns_ref.shape
    for block, row_ref in enumerate(row_refs):
        lanes = slice(128 * block, 128 * block + 128)
        for col in range(cols):
            row_ref[pl.ds(col, rows, stride=cols), :] = columns_ref[col, :, lanes].astype(
                jnp.float32
            )
        flat_ref[:, lanes] = row_ref[...].astype(jnp.bfloat16)
    count, _, size = slices_ref.shape
    part = size // count
    source = lax.broadcasted_iota(jnp.int32, (size, size), 0)
    target = lax.broadcasted_iota(jnp.int32, (size, size), 1)
    wanted = (source % count) * part + source // count
    picker = jnp.where(target == wanted, 1.0, 0.0).astype(jnp.bfloat16)
    sorted_blocks = [
        multiply(flat_ref[:, size * b : size * (b + 1)], picker).astype(jnp.bfloat16)
        for b in range(count)
    ]
    for a in range(count):
        slices_ref[a] = jnp.concatenate(
            [block[:, part * a : part * (a + 1)] for block in sorted_blocks], axis=1
        )


def channel_slices(features):
    rows, cols, in_width = features.shape
    pixels = rows * cols
    return pl.pallas_call(
        slices_kernel,
        out_shape=(
            like((pixels, in_width), jnp.bfloat16),
            like((LAT_COUNT, pixels, in_width // LAT_COUNT), jnp.bfloat16),
        ),
        in_specs=[VMEM],
        out_specs=(VMEM,) * 2,
        scratch_shapes=[pltpu.VMEM((pixels, 128), jnp.float32)] * (in_width // 128),
        compiler_params=params(),
        cost_estimate=cost(2 * pixels * in_width * in_width // LAT_COUNT, 6 * pixels * in_width),
    )(jnp.swapaxes(features, 0, 1))


def row_sum_kernel(
    level_ref,
    below_near_ref,
    below_far_ref,
    above_near_ref,
    above_far_ref,
    west_ref,
    east_ref,
    center_ref,
):
    width = center_ref.shape[1]
    near, far = below_near_ref.shape[0], below_far_ref.shape[0]
    f32 = jnp.float32
    below = jnp.concatenate([below_near_ref[...].astype(f32), below_far_ref[...].astype(f32)])
    above = jnp.concatenate([above_far_ref[...].astype(f32), above_near_ref[...].astype(f32)])
    total = level_ref[...] + below + above
    west_ref[...] = total[:, :width].astype(jnp.bfloat16)
    center_ref[...] = total[:, width : 2 * width]
    east_ref[...] = total[:, 2 * width :].astype(jnp.bfloat16)


def row_sum(level, received):
    pixels, wide = level.shape
    side = like((pixels, wide // 3), jnp.bfloat16)
    return pl.pallas_call(
        row_sum_kernel,
        out_shape=(
            side,
            side,
            like((pixels, wide // 3), jnp.float32),
        ),
        in_specs=[VMEM] * 5,
        out_specs=(VMEM,) * 3,
        compiler_params=params(),
        cost_estimate=cost(3 * pixels * wide, 8 * pixels * wide),
    )(level, *received)


def head_kernel(
    place_ref,
    point_ref,
    center_ref,
    from_east_ref,
    from_west_ref,
    project_ref,
    upstream_ref,
    pixel_weight_ref,
    head_ref,
    grads_ref,
    message_ref,
    mine_ref,
    *terms_refs,
):
    bf16, f32 = jnp.bfloat16, jnp.float32
    width = point_ref.shape[1]
    xh = place_ref[2]
    pre_list = [
        point_ref[...],
        center_ref[...] + from_east_ref[...].astype(f32) + from_west_ref[...].astype(f32),
    ]
    gates = [sigmoid(pre) for pre in pre_list]
    acts = [(pre * gate).astype(bf16) for pre, gate in zip(pre_list, gates)]
    mixed = multiply(acts[0], project_ref[0]) + multiply(acts[1], project_ref[1])
    gate = sigmoid(mixed)
    out = mixed * gate
    cols, rows, _ = head_ref.shape
    for half, row_ref in enumerate(terms_refs):
        lanes = slice(128 * half, 128 * half + 128)
        row_ref[: cols * rows, :] = out[:, lanes]
        for col in range(cols):
            head_ref[col, :, lanes] = row_ref[pl.ds(col, rows, stride=cols), :].astype(bf16)
    slope = gate * (1.0 + mixed * (1.0 - gate))
    out_grad = (upstream_ref[...].astype(f32) * pixel_weight_ref[...] * slope).astype(bf16)
    grads = [
        (
            multiply_transposed(out_grad, project_ref[k])
            * (gates[k] * (1.0 + pre_list[k] * (1.0 - gates[k])))
        ).astype(bf16)
        for k in range(2)
    ]
    pixels = grads_ref.shape[0]
    grads_ref[:, :width] = grads[1]
    grads_ref[:, width:] = grads[0]
    message_ref[:pixels, :width] = grads[1]
    message_ref[:pixels, width:] = grads[0]
    for k in range(2):
        terms = contract_row_axes(acts[k], out_grad)
        for half, terms_ref in enumerate(terms_refs):
            terms_ref[width * k : width * (k + 1), :] = terms[:, 128 * half : 128 * half + 128]
    count, part, _ = mine_ref.shape
    for y in range(count):
        rows = slice(pixels + y % 2 * part, pixels + y % 2 * part + part)
        for half, terms_ref in enumerate(terms_refs):
            even = terms_ref[pl.ds(2 * y, part, stride=2 * count), :]
            odd = terms_ref[pl.ds(2 * y + 1, part, stride=2 * count), :]
            lanes = slice(128 * half, 128 * half + 128)
            mine_ref[y, :, lanes] = jnp.where(xh == 0, even, odd)
            low = y // 2 * width + 128 * half
            message_ref[rows, low : low + 128] = jnp.where(xh == 0, odd, even).astype(bf16)


def head(
    rows, place, point_pre, center, from_east, from_west, project, upstream, pixel_weight
):
    pixels, width = point_pre.shape
    count = AXIS_SIZES["y"]
    part = width // count
    bf16, f32 = jnp.bfloat16, jnp.float32
    return pl.pallas_call(
        head_kernel,
        out_shape=(
            like((pixels // rows, rows, width), bf16),
            like((pixels, 2 * width), bf16),
            like((pixels + 2 * part, 2 * width), bf16),
            like((count, part, width), f32),
        ),
        in_specs=[SMEM] + [VMEM] * 7,
        out_specs=(VMEM,) * 4,
        scratch_shapes=[pltpu.VMEM((2 * width, 128), f32)] * (width // 128),
        compiler_params=params(),
        cost_estimate=cost(12 * pixels * width * width, 24 * pixels * width),
    )(place, point_pre, center, from_east, from_west, project, upstream, pixel_weight)


def forward_kernel(
    grads_ref,
    received_ref,
    mine_ref,
    *refs,
):
    message_ref = refs[-2]
    count, part, width = mine_ref.shape
    pixels = grads_ref.shape[0]
    for at in range(count):
        for slot, piece_ref in enumerate((grads_ref, received_ref)):
            for k in (0, 1):
                first = (2 * slot + k) * pixels
                message_ref[at, first : first + pixels, :] = piece_ref[
                    :pixels, k * width : (k + 1) * width
                ]
        rows = slice(pixels + at % 2 * part, pixels + at % 2 * part + part)
        low = at // 2 * width
        terms = mine_ref[at] + received_ref[rows, low : low + width].astype(jnp.float32)
        message_ref[at, 4 * pixels :, :] = terms.astype(jnp.bfloat16)


def forward(grads, received, mine, after, features):
    count, part, width = mine.shape
    pixels = grads.shape[0]
    return pl.pallas_call(
        forward_kernel,
        out_shape=(
            like((count, 4 * pixels + part, width), jnp.bfloat16),
            like(features.shape, features.dtype),
        ),
        in_specs=[VMEM] * 3 + [ANY] * 5,
        out_specs=(VMEM, ANY),
        input_output_aliases={7: 1},
        compiler_params=params(),
        cost_estimate=cost(mine.size, 8 * received.size),
    )(grads, received, mine, *after, features)


def weight_terms_kernel(
    span,
    chunk,
    place_ref,
    center_in_ref,
    east_first_ref,
    east_second_ref,
    west_first_ref,
    west_second_ref,
    message_in_ref,
    kept_ref,
    rounded_ref,
    windows_ref,
    framed_ref,
    features_ref,
    message_ref,
    sent_ref,
    semaphores,
):
    _, total, width = features_ref.shape
    first_rows = east_first_ref.shape[0]
    message_copy = pltpu.make_async_copy(message_in_ref, message_ref, semaphores.at[0])
    copies = {
        0: [pltpu.make_async_copy(center_in_ref, features_ref.at[0], semaphores.at[1])],
        1: [
            pltpu.make_async_copy(
                east_first_ref, features_ref.at[1, pl.ds(0, first_rows)], semaphores.at[2]
            ),
            pltpu.make_async_copy(
                east_second_ref,
                features_ref.at[1, pl.ds(first_rows, total - first_rows)],
                semaphores.at[3],
            ),
        ],
        -1: [
            pltpu.make_async_copy(
                west_first_ref, features_ref.at[2, pl.ds(0, first_rows)], semaphores.at[4]
            ),
            pltpu.make_async_copy(
                west_second_ref,
                features_ref.at[2, pl.ds(first_rows, total - first_rows)],
                semaphores.at[5],
            ),
        ],
    }
    message_copy.start()
    for j in (0, 1, -1):
        for copy in copies[j]:
            copy.start()
    pixels = total // LAT_COUNT
    room = padded(chunk)
    core, y, xh = place_ref[0], place_ref[1], place_ref[2]

    edge = jnp.zeros((span, width), framed_ref.dtype)
    framed_ref[total : total + span, :width] = edge
    framed_ref[span : 2 * span, 2 * width : 3 * width] = edge
    message_copy.wait()
    for at in range(message_ref.shape[0]):
        for slot in (0, 1):
            band = 2 * at + (xh + slot) % 2
            low = 2 * slot * pixels
            piece = message_ref[at, low : low + pixels, :]
            for i in (-1, 0, 1):
                first = pl.multiple_of(span + span * i + band * pixels, 16)
                framed_ref[pl.ds(first, pixels), (i + 1) * width : (i + 2) * width] = piece
            first = pl.multiple_of(span + band * pixels, 16)
            framed_ref[pl.ds(first, pixels), 3 * width :] = message_ref[
                at, low + pixels : low + 2 * pixels, :
            ]
    own_rows = pl.ds(pl.multiple_of(span + (2 * y + xh) * pixels, 16), pixels)
    windows_ref[...] = framed_ref[own_rows, : 3 * width]

    def store(first, value):
        count = value.shape[0]
        pieces = []
        at = 0
        while at < count:
            index, offset = divmod(first + at, chunk)
            size = min(chunk - offset, count - at)
            pieces.append((index, offset, at, size))
            at += size
        for owner in (0, 1):

            @pl.when(core == owner)
            def _():
                for index, offset, at, size in pieces:
                    target = kept_ref if index % 2 == owner else sent_ref
                    first_row = index // 2 * room + offset
                    target[first_row : first_row + size, :] = value[at : at + size]

    for j in (0, 1, -1):
        wide = 4 * width if j == 0 else 3 * width
        for copy in copies[j]:
            copy.wait()
        product = contract_row_axes(features_ref[j % 3], framed_ref[span : span + total, :wide])
        for i in (-1, 0, 1):
            store((3 * (i + 1) + j + 1) * width, product[:, (i + 1) * width : (i + 2) * width])
        if j == 0:
            project_rows = jnp.sum(message_ref[:, 4 * pixels :, :].astype(jnp.float32), axis=0)
            store(9 * width, project_rows)
            store(9 * width + project_rows.shape[0], product[:, 3 * width :])
    rounded_ref[...] = sent_ref[...].astype(rounded_ref.dtype)


def padded(chunk):
    return (chunk + 15) // 16 * 16


def weight_terms(span, place, features, message):
    total, width = features[0].shape
    pixels = total // LAT_COUNT
    chunk = (10 * width + message.shape[1] - 4 * pixels) // LON_COUNT
    terms_shape = (LON_COUNT // 2 * padded(chunk), width)
    return pl.pallas_call(
        functools.partial(weight_terms_kernel, span, chunk),
        out_shape=(
            like(terms_shape, jnp.float32),
            like(terms_shape, jnp.bfloat16),
            like((pixels, 3 * width), jnp.bfloat16),
        ),
        in_specs=[SMEM] + [ANY] * 6,
        out_specs=(VMEM,) * 3,
        scratch_shapes=[
            pltpu.VMEM((2 * span + total, 4 * width), jnp.bfloat16),
            pltpu.VMEM((3, total, width), jnp.bfloat16),
            pltpu.VMEM(message.shape, jnp.bfloat16),
            pltpu.VMEM(terms_shape, jnp.float32),
            pltpu.SemaphoreType.DMA((6,)),
        ],
        compiler_params=params(60),
        cost_estimate=cost(20 * total * width * width, 8 * 2**20),
    )(place, *features, message)


def pair_sum_kernel(kept_ref, received_ref, out_ref):
    count, chunk, _ = out_ref.shape
    room = kept_ref.shape[0] // count
    for at in range(count):
        rows = slice(room * at, room * (at + 1))
        total = kept_ref[rows, :] + received_ref[rows, :].astype(jnp.float32)
        out_ref[at] = total[:chunk].astype(jnp.bfloat16)


def pair_sum(kept, received, chunk):
    return pl.pallas_call(
        pair_sum_kernel,
        out_shape=like((LON_COUNT // 2, chunk, kept.shape[1]), jnp.bfloat16),
        in_specs=[VMEM] * 2,
        out_specs=VMEM,
        compiler_params=params(),
        cost_estimate=cost(kept.size, 10 * kept.size),
    )(kept, received)


def side_slices_kernel(
    east_grad_ref, west_grad_ref, up_near_ref, up_far_ref, down_near_ref, down_far_ref
):
    far = up_far_ref.shape[0]
    for at, side_ref in enumerate((east_grad_ref, west_grad_ref)):
        side = side_ref[...]
        pixels, width = side.shape
        lanes = slice(at * width, (at + 1) * width)
        up_near_ref[:, lanes] = side[far:]
        up_far_ref[:, lanes] = side[:far]
        down_near_ref[:, lanes] = side[: pixels - far]
        down_far_ref[:, lanes] = side[pixels - far :]


def side_slices(east_grad, west_grad, far):
    pixels, width = east_grad.shape
    near_shape = like((pixels - far, 2 * width), jnp.bfloat16)
    far_shape = like((far, 2 * width), jnp.bfloat16)
    return pl.pallas_call(
        side_slices_kernel,
        out_shape=(near_shape, far_shape, near_shape, far_shape),
        in_specs=[VMEM] * 2,
        out_specs=(VMEM,) * 4,
        compiler_params=params(),
        cost_estimate=cost(pixels * width, 8 * pixels * width),
    )(east_grad, west_grad)


def piece_sum_kernel(pieces_ref, *refs):
    out_ref = refs[-1]
    total = pieces_ref[0].astype(jnp.float32)
    for at in range(1, pieces_ref.shape[0]):
        total = total + pieces_ref[at].astype(jnp.float32)
    rounded = total.astype(out_ref.dtype)
    for at in range(out_ref.shape[0]):
        out_ref[at] = rounded


def piece_sum(pieces, after):
    return pl.pallas_call(
        piece_sum_kernel,
        out_shape=like((LAT_COUNT,) + pieces.shape[1:], jnp.bfloat16),
        in_specs=[VMEM] + [ANY] * len(after),
        out_specs=VMEM,
        compiler_params=params(),
        cost_estimate=cost(pieces.size, 4 * pieces.size),
    )(pieces, *after)


def interleave_kernel(parts_ref, out_ref, *sorted_refs):
    count, size, _ = parts_ref.shape
    for half, sorted_ref in enumerate(sorted_refs):
        lanes = slice(128 * half, 128 * half + 128)
        for a in range(count):
            sorted_ref[pl.ds(a, size, stride=count), :] = parts_ref[a, :, lanes].astype(
                jnp.float32
            )
        out_ref[:, lanes] = sorted_ref[...]


def interleave(parts):
    count, size, width = parts.shape
    return pl.pallas_call(
        interleave_kernel,
        out_shape=like((count * size, width), jnp.float32),
        in_specs=[VMEM],
        out_specs=VMEM,
        scratch_shapes=[pltpu.VMEM((count * size, 128), jnp.float32)] * (width // 128),
        compiler_params=params(),
        cost_estimate=cost(parts.size, 8 * parts.size),
    )(parts)


def add_product(total_ref, window, tap_ref, first):
    size = 512
    for low in range(0, total_ref.shape[1], size):
        lanes = slice(low, low + size)
        product = multiply_transposed(window, tap_ref[low : low + size, :])
        total_ref[:, lanes] = product if first else total_ref[:, lanes] + product


def input_gradient_kernel(
    windows_ref,
    grads_ref,
    east_ref,
    west_ref,
    up_near_ref,
    up_far_ref,
    down_near_ref,
    down_far_ref,
    kernel_ref,
    point_weight_ref,
    out_ref,
    total_ref,
    buffer_ref,
    semaphores,
    *row_refs,
):
    width = buffer_ref.shape[2]
    cols, rows, _ = out_ref.shape
    sources = [point_weight_ref] + [kernel_ref.at[tap] for tap in (1, 4, 7, 2, 5, 8, 0, 3, 6)]
    for at, tap_ref in enumerate(stream(sources, buffer_ref, semaphores)):
        side, i = divmod(at - 4, 3)
        lanes = slice(side * width, (side + 1) * width)
        if at == 0:
            window = grads_ref[:, width:]
        elif at < 4:
            window = windows_ref[:, (at - 1) * width : at * width]
        elif i == 0:
            window = jnp.concatenate([up_near_ref[:, lanes], up_far_ref[:, lanes]])
        elif i == 1:
            window = (east_ref, west_ref)[side][...]
        else:
            window = jnp.concatenate([down_far_ref[:, lanes], down_near_ref[:, lanes]])
        add_product(total_ref, window, tap_ref, at == 0)
    for block, row_ref in enumerate(row_refs):
        lanes = slice(128 * block, 128 * block + 128)
        row_ref[...] = total_ref[:, lanes]
        for col in range(cols):
            out_ref[col, :, lanes] = row_ref[pl.ds(col, rows, stride=cols), :].astype(out_ref.dtype)


def input_gradient(rows, windows, grads, east, west, side_rows, kernel, point_weight):
    pixels = grads.shape[0]
    in_width, width = point_weight.shape
    return pl.pallas_call(
        input_gradient_kernel,
        out_shape=like((pixels // rows, rows, in_width), jnp.bfloat16),
        in_specs=[VMEM] * 8 + [ANY] * 2,
        out_specs=VMEM,
        scratch_shapes=[pltpu.VMEM((pixels, in_width), jnp.float32)]
        + stream_scratch(in_width, width)
        + [pltpu.VMEM((pixels, 128), jnp.float32)] * (in_width // 128),
        compiler_params=params(60),
        cost_estimate=cost(20 * pixels * in_width * width, 40 * in_width * width),
    )(windows, grads, east, west, *side_rows, kernel, point_weight)


def shards(features, kernel, point_weight, project_weight, upstream, labels, class_weights):
    rows, cols, in_width = features.shape
    width = point_weight.shape[1]
    pixels = rows * cols
    place = jnp.stack([lax.axis_index("c"), lax.axis_index("y"), lax.axis_index("xh")])
    near = ATROUS_DILATION // rows
    far_pixels = (ATROUS_DILATION - near * rows) * cols
    tiles_over = ATROUS_DILATION // cols
    span = ATROUS_DILATION * cols

    flat, slices = channel_slices(features)
    below_near, below_far, above_near, above_far, level, point_pre = tap_products(
        flat, kernel, point_weight, far_pixels, slices
    )
    received = (
        shift_rows(below_near, -near),
        shift_rows(below_far, -(near + 1)),
        shift_rows(above_near, near),
        shift_rows(above_far, near + 1),
    )
    column_features = lax.all_to_all(slices, LAT, 0, 0).reshape(LAT_COUNT * pixels, -1)
    first_rows = FIRST_BANDS * pixels
    first_features, second_features = column_features[:first_rows], column_features[first_rows:]
    to_east, to_west, center = row_sum(level, received)
    from_east = shift_columns(to_west, -tiles_over)
    from_west = shift_columns(to_east, tiles_over)
    class_index = jnp.arange(3, dtype=jnp.int32)
    pixel_weight = jnp.sum(
        jnp.where(labels[..., None] == class_index, class_weights, 0.0), axis=-1
    ).reshape(-1, 1)
    head_out, grads, message, mine = head(
        rows,
        place,
        point_pre,
        center,
        from_east,
        from_west,
        project_weight,
        upstream.reshape(pixels, width),
        pixel_weight,
    )

    other = lax.ppermute(message, "xh", [(0, 1), (1, 0)])
    first_east = shift_columns(first_features, -tiles_over)
    first_west = shift_columns(first_features, tiles_over)
    east_grad = shift_columns(grads[:, :width], tiles_over)
    west_grad = shift_columns(grads[:, :width], -tiles_over)
    message, second_features = forward(
        grads, other, mine, (first_east, first_west, east_grad, west_grad), second_features
    )
    gathered = lax.all_to_all(message, "y", 0, 0)
    second_east = shift_columns(second_features, -tiles_over)
    second_west = shift_columns(second_features, tiles_over)

    kept, sent, windows = weight_terms(
        span,
        place,
        (column_features, first_east, second_east, first_west, second_west),
        gathered,
    )
    chunk = (10 * in_width + 2 * width) // (LAT_COUNT * LON_COUNT)
    chip_sum = pair_sum(kept, lax.ppermute(sent, "c", [(0, 1), (1, 0)]), chunk)
    up_near, up_far, down_near, down_far = side_slices(east_grad, west_grad, far_pixels)
    side_rows = (
        shift_rows(up_near, -near),
        shift_rows(up_far, -(near + 1)),
        shift_rows(down_near, near),
        shift_rows(down_far, near + 1),
    )
    pieces = lax.all_to_all(chip_sum, ("xl", "z"), 0, 0)

    weight_grads = interleave(lax.all_to_all(piece_sum(pieces, side_rows), LAT, 0, 0))
    input_grad = input_gradient(
        rows, windows, grads, east_grad, west_grad, side_rows, kernel, point_weight
    )

    head_tile = jnp.swapaxes(head_out, 0, 1)
    grad_tile = jnp.swapaxes(input_grad, 0, 1)
    return (head_tile, grad_tile, weight_grads)


def solution(mesh):
    split = Mesh(mesh.devices.reshape(tuple(AXIS_SIZES.values())), tuple(AXIS_SIZES))
    tile = P(LAT, LON, None)
    return jax.shard_map(
        shards,
        mesh=split,
        in_specs=(tile, P(), P(), P(), tile, P(LAT, LON), P()),
        out_specs=(tile, tile, P(LON, None)),
        check_vma=False,
    )
```

```python
import functools

import jax
import jax.numpy as jnp
from jax import lax
from jax.experimental import pallas as pl
from jax.experimental.pallas import tpu as pltpu
from jax.sharding import Mesh, PartitionSpec as P

ATROUS_DILATION = 36
LAT = ("y", "xh")
LON = ("xl", "z", "c")
AXIS_SIZES = {"y": 4, "xh": 2, "xl": 2, "z": 8, "c": 2}
LAT_COUNT = 8
LON_COUNT = 32
FIRST_BANDS = 4
VMEM = pl.BlockSpec(memory_space=pltpu.VMEM)
SMEM = pl.BlockSpec(memory_space=pltpu.SMEM)
ANY = pl.BlockSpec(memory_space=pl.ANY)


def shift_rows(value, by):
    pairs = [(i, i + by) for i in range(LAT_COUNT) if 0 <= i + by < LAT_COUNT]
    return lax.ppermute(value, LAT, pairs)


def shift_columns(value, by):
    return lax.ppermute(value, LON, [(i, (i + by) % LON_COUNT) for i in range(LON_COUNT)])


def contract_row_axes(left, right):
    return lax.dot_general(
        left, right, (((0,), (0,)), ((), ())), preferred_element_type=jnp.float32
    )


def multiply_transposed(left, right):
    return lax.dot_general(
        left, right, (((1,), (1,)), ((), ())), preferred_element_type=jnp.float32
    )


def multiply(left, right):
    return jnp.dot(left, right, preferred_element_type=jnp.float32)


def sigmoid(value):
    return 1.0 / (1.0 + jnp.exp(-value))


def params(megabytes=24):
    return pltpu.CompilerParams(vmem_limit_bytes=megabytes * 2**20)


def cost(flops, moved):
    return pl.CostEstimate(flops=int(flops), bytes_accessed=int(moved), transcendentals=0)


def like(shape, dtype):
    return jax.ShapeDtypeStruct(shape, dtype)


def stream(sources, buffer_ref, semaphores):
    depth = buffer_ref.shape[0]

    def copy(at):
        return pltpu.make_async_copy(
            sources[at], buffer_ref.at[at % depth], semaphores.at[at % depth]
        )

    for at in range(min(depth - 1, len(sources))):
        copy(at).start()
    for at in range(len(sources)):
        if at + depth - 1 < len(sources):
            copy(at + depth - 1).start()
        copy(at).wait()
        yield buffer_ref.at[at % depth]


STREAM_DEPTH = 6


def stream_scratch(in_width, width):
    return [
        pltpu.VMEM((STREAM_DEPTH, in_width, width), jnp.bfloat16),
        pltpu.SemaphoreType.DMA((STREAM_DEPTH,)),
    ]


def products_kernel(
    flat_ref,
    kernel_ref,
    point_weight_ref,
    after_ref,
    below_near_ref,
    below_far_ref,
    above_near_ref,
    above_far_ref,
    level_ref,
    point_ref,
):
    width = kernel_ref.shape[2]
    pixels = flat_ref.shape[0]
    far = below_far_ref.shape[0]
    for at, tap in enumerate((6, 7, 8, 0, 1, 2, 3, 4, 5)):
        product = multiply(flat_ref[...], kernel_ref[tap])
        rounded = product.astype(jnp.bfloat16)
        lanes = slice((at % 3) * width, (at % 3 + 1) * width)
        if at < 3:
            below_far_ref[:, lanes] = rounded[:far]
            below_near_ref[:, lanes] = rounded[far:]
        elif at < 6:
            above_near_ref[:, lanes] = rounded[: pixels - far]
            above_far_ref[:, lanes] = rounded[pixels - far :]
        else:
            level_ref[:, lanes] = product
    point_ref[...] = multiply(flat_ref[...], point_weight_ref[...])


def tap_products(flat, kernel, point_weight, far, after):
    pixels, in_width = flat.shape
    width = kernel.shape[2]
    near_shape = like((pixels - far, 3 * width), jnp.bfloat16)
    far_shape = like((far, 3 * width), jnp.bfloat16)
    return pl.pallas_call(
        products_kernel,
        out_shape=(near_shape, far_shape, near_shape, far_shape)
        + (like((pixels, 3 * width), jnp.float32), like((pixels, width), jnp.float32)),
        in_specs=[VMEM] * 3 + [ANY],
        out_specs=(VMEM,) * 6,
        compiler_params=params(),
        cost_estimate=cost(20 * pixels * in_width * width, 20 * in_width * width),
    )(flat, kernel, point_weight, after)


def slices_kernel(columns_ref, flat_ref, slices_ref, *row_refs):
    cols, rows, _ = columns_ref.shape
    for block, row_ref in enumerate(row_refs):
        lanes = slice(128 * block, 128 * block + 128)
        for col in range(cols):
            row_ref[pl.ds(col, rows, stride=cols), :] = columns_ref[col, :, lanes].astype(
                jnp.float32
            )
        flat_ref[:, lanes] = row_ref[...].astype(jnp.bfloat16)
    count, _, size = slices_ref.shape
    part = size // count
    source = lax.broadcasted_iota(jnp.int32, (size, size), 0)
    target = lax.broadcasted_iota(jnp.int32, (size, size), 1)
    wanted = (source % count) * part + source // count
    picker = jnp.where(target == wanted, 1.0, 0.0).astype(jnp.bfloat16)
    sorted_blocks = [
        multiply(flat_ref[:, size * b : size * (b + 1)], picker).astype(jnp.bfloat16)
        for b in range(count)
    ]
    for a in range(count):
        slices_ref[a] = jnp.concatenate(
            [block[:, part * a : part * (a + 1)] for block in sorted_blocks], axis=1
        )


def channel_slices(features):
    rows, cols, in_width = features.shape
    pixels = rows * cols
    return pl.pallas_call(
        slices_kernel,
        out_shape=(
            like((pixels, in_width), jnp.bfloat16),
            like((LAT_COUNT, pixels, in_width // LAT_COUNT), jnp.bfloat16),
        ),
        in_specs=[VMEM],
        out_specs=(VMEM,) * 2,
        scratch_shapes=[pltpu.VMEM((pixels, 128), jnp.float32)] * (in_width // 128),
        compiler_params=params(),
        cost_estimate=cost(2 * pixels * in_width * in_width // LAT_COUNT, 6 * pixels * in_width),
    )(jnp.swapaxes(features, 0, 1))


def row_sum_kernel(
    level_ref,
    below_near_ref,
    below_far_ref,
    above_near_ref,
    above_far_ref,
    west_ref,
    east_ref,
    center_ref,
):
    width = center_ref.shape[1]
    near, far = below_near_ref.shape[0], below_far_ref.shape[0]
    f32 = jnp.float32
    below = jnp.concatenate([below_near_ref[...].astype(f32), below_far_ref[...].astype(f32)])
    above = jnp.concatenate([above_far_ref[...].astype(f32), above_near_ref[...].astype(f32)])
    total = level_ref[...] + below + above
    west_ref[...] = total[:, :width].astype(jnp.bfloat16)
    center_ref[...] = total[:, width : 2 * width]
    east_ref[...] = total[:, 2 * width :].astype(jnp.bfloat16)


def row_sum(level, received):
    pixels, wide = level.shape
    side = like((pixels, wide // 3), jnp.bfloat16)
    return pl.pallas_call(
        row_sum_kernel,
        out_shape=(
            side,
            side,
            like((pixels, wide // 3), jnp.float32),
        ),
        in_specs=[VMEM] * 5,
        out_specs=(VMEM,) * 3,
        compiler_params=params(),
        cost_estimate=cost(3 * pixels * wide, 8 * pixels * wide),
    )(level, *received)


def head_kernel(
    place_ref,
    point_ref,
    center_ref,
    from_east_ref,
    from_west_ref,
    project_ref,
    upstream_ref,
    pixel_weight_ref,
    head_ref,
    grads_ref,
    message_ref,
    mine_ref,
    *terms_refs,
):
    bf16, f32 = jnp.bfloat16, jnp.float32
    width = point_ref.shape[1]
    xh = place_ref[2]
    pre_list = [
        point_ref[...],
        center_ref[...] + from_east_ref[...].astype(f32) + from_west_ref[...].astype(f32),
    ]
    gates = [sigmoid(pre) for pre in pre_list]
    acts = [(pre * gate).astype(bf16) for pre, gate in zip(pre_list, gates)]
    mixed = multiply(acts[0], project_ref[0]) + multiply(acts[1], project_ref[1])
    gate = sigmoid(mixed)
    out = mixed * gate
    cols, rows, _ = head_ref.shape
    for half, row_ref in enumerate(terms_refs):
        lanes = slice(128 * half, 128 * half + 128)
        row_ref[: cols * rows, :] = out[:, lanes]
        for col in range(cols):
            head_ref[col, :, lanes] = row_ref[pl.ds(col, rows, stride=cols), :].astype(bf16)
    slope = gate * (1.0 + mixed * (1.0 - gate))
    out_grad = (upstream_ref[...].astype(f32) * pixel_weight_ref[...] * slope).astype(bf16)
    grads = [
        (
            multiply_transposed(out_grad, project_ref[k])
            * (gates[k] * (1.0 + pre_list[k] * (1.0 - gates[k])))
        ).astype(bf16)
        for k in range(2)
    ]
    pixels = grads_ref.shape[0]
    grads_ref[:, :width] = grads[1]
    grads_ref[:, width:] = grads[0]
    message_ref[:pixels, :width] = grads[1]
    message_ref[:pixels, width:] = grads[0]
    for k in range(2):
        terms = contract_row_axes(acts[k], out_grad)
        for half, terms_ref in enumerate(terms_refs):
            terms_ref[width * k : width * (k + 1), :] = terms[:, 128 * half : 128 * half + 128]
    count, part, _ = mine_ref.shape
    for y in range(count):
        rows = slice(pixels + y % 2 * part, pixels + y % 2 * part + part)
        for half, terms_ref in enumerate(terms_refs):
            even = terms_ref[pl.ds(2 * y, part, stride=2 * count), :]
            odd = terms_ref[pl.ds(2 * y + 1, part, stride=2 * count), :]
            lanes = slice(128 * half, 128 * half + 128)
            mine_ref[y, :, lanes] = jnp.where(xh == 0, even, odd)
            low = y // 2 * width + 128 * half
            message_ref[rows, low : low + 128] = jnp.where(xh == 0, odd, even).astype(bf16)


def head(
    rows, place, point_pre, center, from_east, from_west, project, upstream, pixel_weight
):
    pixels, width = point_pre.shape
    count = AXIS_SIZES["y"]
    part = width // count
    bf16, f32 = jnp.bfloat16, jnp.float32
    return pl.pallas_call(
        head_kernel,
        out_shape=(
            like((pixels // rows, rows, width), bf16),
            like((pixels, 2 * width), bf16),
            like((pixels + 2 * part, 2 * width), bf16),
            like((count, part, width), f32),
        ),
        in_specs=[SMEM] + [VMEM] * 7,
        out_specs=(VMEM,) * 4,
        scratch_shapes=[pltpu.VMEM((2 * width, 128), f32)] * (width // 128),
        compiler_params=params(),
        cost_estimate=cost(12 * pixels * width * width, 24 * pixels * width),
    )(place, point_pre, center, from_east, from_west, project, upstream, pixel_weight)


def forward_kernel(
    grads_ref,
    received_ref,
    mine_ref,
    *refs,
):
    message_ref = refs[-2]
    count, part, width = mine_ref.shape
    pixels = grads_ref.shape[0]
    for at in range(count):
        for slot, piece_ref in enumerate((grads_ref, received_ref)):
            for k in (0, 1):
                first = (2 * slot + k) * pixels
                message_ref[at, first : first + pixels, :] = piece_ref[
                    :pixels, k * width : (k + 1) * width
                ]
        rows = slice(pixels + at % 2 * part, pixels + at % 2 * part + part)
        low = at // 2 * width
        terms = mine_ref[at] + received_ref[rows, low : low + width].astype(jnp.float32)
        message_ref[at, 4 * pixels :, :] = terms.astype(jnp.bfloat16)


def forward(grads, received, mine, after, features):
    count, part, width = mine.shape
    pixels = grads.shape[0]
    return pl.pallas_call(
        forward_kernel,
        out_shape=(
            like((count, 4 * pixels + part, width), jnp.bfloat16),
            like(features.shape, features.dtype),
        ),
        in_specs=[VMEM] * 3 + [ANY] * 5,
        out_specs=(VMEM, ANY),
        input_output_aliases={7: 1},
        compiler_params=params(),
        cost_estimate=cost(mine.size, 8 * received.size),
    )(grads, received, mine, *after, features)


def weight_terms_kernel(
    span,
    chunk,
    place_ref,
    center_in_ref,
    east_first_ref,
    east_second_ref,
    west_first_ref,
    west_second_ref,
    message_in_ref,
    rounded_kept_ref,
    rounded_sent_ref,
    windows_ref,
    framed_ref,
    features_ref,
    message_ref,
    kept_ref,
    sent_ref,
    semaphores,
):
    _, total, width = features_ref.shape
    first_rows = east_first_ref.shape[0]
    message_copy = pltpu.make_async_copy(message_in_ref, message_ref, semaphores.at[0])
    copies = {
        0: [pltpu.make_async_copy(center_in_ref, features_ref.at[0], semaphores.at[1])],
        1: [
            pltpu.make_async_copy(
                east_first_ref, features_ref.at[1, pl.ds(0, first_rows)], semaphores.at[2]
            ),
            pltpu.make_async_copy(
                east_second_ref,
                features_ref.at[1, pl.ds(first_rows, total - first_rows)],
                semaphores.at[3],
            ),
        ],
        -1: [
            pltpu.make_async_copy(
                west_first_ref, features_ref.at[2, pl.ds(0, first_rows)], semaphores.at[4]
            ),
            pltpu.make_async_copy(
                west_second_ref,
                features_ref.at[2, pl.ds(first_rows, total - first_rows)],
                semaphores.at[5],
            ),
        ],
    }
    message_copy.start()
    for j in (0, 1, -1):
        for copy in copies[j]:
            copy.start()
    pixels = total // LAT_COUNT
    room = padded(chunk)
    core, y, xh = place_ref[0], place_ref[1], place_ref[2]

    edge = jnp.zeros((span, width), framed_ref.dtype)
    framed_ref[total : total + span, :width] = edge
    framed_ref[span : 2 * span, 2 * width : 3 * width] = edge
    message_copy.wait()
    for at in range(message_ref.shape[0]):
        for slot in (0, 1):
            band = 2 * at + (xh + slot) % 2
            low = 2 * slot * pixels
            piece = message_ref[at, low : low + pixels, :]
            for i in (-1, 0, 1):
                first = pl.multiple_of(span + span * i + band * pixels, 16)
                framed_ref[pl.ds(first, pixels), (i + 1) * width : (i + 2) * width] = piece
            first = pl.multiple_of(span + band * pixels, 16)
            framed_ref[pl.ds(first, pixels), 3 * width :] = message_ref[
                at, low + pixels : low + 2 * pixels, :
            ]
    own_rows = pl.ds(pl.multiple_of(span + (2 * y + xh) * pixels, 16), pixels)
    windows_ref[...] = framed_ref[own_rows, : 3 * width]

    def store(first, value):
        count = value.shape[0]
        pieces = []
        at = 0
        while at < count:
            index, offset = divmod(first + at, chunk)
            size = min(chunk - offset, count - at)
            pieces.append((index, offset, at, size))
            at += size
        for owner in (0, 1):

            @pl.when(core == owner)
            def _():
                for index, offset, at, size in pieces:
                    target = kept_ref if index % 2 == owner else sent_ref
                    first_row = index // 2 * room + offset
                    target[first_row : first_row + size, :] = value[at : at + size]

    for j in (0, 1, -1):
        wide = 4 * width if j == 0 else 3 * width
        for copy in copies[j]:
            copy.wait()
        product = contract_row_axes(features_ref[j % 3], framed_ref[span : span + total, :wide])
        for i in (-1, 0, 1):
            store((3 * (i + 1) + j + 1) * width, product[:, (i + 1) * width : (i + 2) * width])
        if j == 0:
            project_rows = jnp.sum(message_ref[:, 4 * pixels :, :].astype(jnp.float32), axis=0)
            store(9 * width, project_rows)
            store(9 * width + project_rows.shape[0], product[:, 3 * width :])
    rounded_kept_ref[...] = kept_ref[...].astype(rounded_kept_ref.dtype)
    rounded_sent_ref[...] = sent_ref[...].astype(rounded_sent_ref.dtype)


def padded(chunk):
    return (chunk + 15) // 16 * 16


def weight_terms(span, place, features, message):
    total, width = features[0].shape
    pixels = total // LAT_COUNT
    chunk = (10 * width + message.shape[1] - 4 * pixels) // LON_COUNT
    terms_shape = (LON_COUNT // 2 * padded(chunk), width)
    return pl.pallas_call(
        functools.partial(weight_terms_kernel, span, chunk),
        out_shape=(
            like(terms_shape, jnp.bfloat16),
            like(terms_shape, jnp.bfloat16),
            like((pixels, 3 * width), jnp.bfloat16),
        ),
        in_specs=[SMEM] + [ANY] * 6,
        out_specs=(VMEM,) * 3,
        scratch_shapes=[
            pltpu.VMEM((2 * span + total, 4 * width), jnp.bfloat16),
            pltpu.VMEM((3, total, width), jnp.bfloat16),
            pltpu.VMEM(message.shape, jnp.bfloat16),
            pltpu.VMEM(terms_shape, jnp.float32),
            pltpu.VMEM(terms_shape, jnp.float32),
            pltpu.SemaphoreType.DMA((6,)),
        ],
        compiler_params=params(60),
        cost_estimate=cost(20 * total * width * width, 8 * 2**20),
    )(place, *features, message)


def pair_sum_kernel(kept_ref, received_ref, out_ref):
    count, chunk, _ = out_ref.shape
    room = kept_ref.shape[0] // count
    for at in range(count):
        rows = slice(room * at, room * (at + 1))
        total = kept_ref[rows, :].astype(jnp.float32) + received_ref[rows, :].astype(
            jnp.float32
        )
        out_ref[at] = total[:chunk].astype(jnp.bfloat16)


def pair_sum(kept, received, chunk):
    return pl.pallas_call(
        pair_sum_kernel,
        out_shape=like((LON_COUNT // 2, chunk, kept.shape[1]), jnp.bfloat16),
        in_specs=[VMEM] * 2,
        out_specs=VMEM,
        compiler_params=params(),
        cost_estimate=cost(kept.size, 10 * kept.size),
    )(kept, received)


def side_slices_kernel(
    east_grad_ref, west_grad_ref, up_near_ref, up_far_ref, down_near_ref, down_far_ref
):
    far = up_far_ref.shape[0]
    for at, side_ref in enumerate((east_grad_ref, west_grad_ref)):
        side = side_ref[...]
        pixels, width = side.shape
        lanes = slice(at * width, (at + 1) * width)
        up_near_ref[:, lanes] = side[far:]
        up_far_ref[:, lanes] = side[:far]
        down_near_ref[:, lanes] = side[: pixels - far]
        down_far_ref[:, lanes] = side[pixels - far :]


def side_slices(east_grad, west_grad, far):
    pixels, width = east_grad.shape
    near_shape = like((pixels - far, 2 * width), jnp.bfloat16)
    far_shape = like((far, 2 * width), jnp.bfloat16)
    return pl.pallas_call(
        side_slices_kernel,
        out_shape=(near_shape, far_shape, near_shape, far_shape),
        in_specs=[VMEM] * 2,
        out_specs=(VMEM,) * 4,
        compiler_params=params(),
        cost_estimate=cost(pixels * width, 8 * pixels * width),
    )(east_grad, west_grad)


def piece_sum_kernel(pieces_ref, *refs):
    out_ref = refs[-1]
    total = pieces_ref[0].astype(jnp.float32)
    for at in range(1, pieces_ref.shape[0]):
        total = total + pieces_ref[at].astype(jnp.float32)
    rounded = total.astype(out_ref.dtype)
    for at in range(out_ref.shape[0]):
        out_ref[at] = rounded


def piece_sum(pieces, after):
    return pl.pallas_call(
        piece_sum_kernel,
        out_shape=like((LAT_COUNT,) + pieces.shape[1:], jnp.bfloat16),
        in_specs=[VMEM] + [ANY] * len(after),
        out_specs=VMEM,
        compiler_params=params(),
        cost_estimate=cost(pieces.size, 4 * pieces.size),
    )(pieces, *after)


def interleave_kernel(parts_ref, out_ref, *sorted_refs):
    count, size, _ = parts_ref.shape
    for half, sorted_ref in enumerate(sorted_refs):
        lanes = slice(128 * half, 128 * half + 128)
        for a in range(count):
            sorted_ref[pl.ds(a, size, stride=count), :] = parts_ref[a, :, lanes].astype(
                jnp.float32
            )
        out_ref[:, lanes] = sorted_ref[...]


def interleave(parts):
    count, size, width = parts.shape
    return pl.pallas_call(
        interleave_kernel,
        out_shape=like((count * size, width), jnp.float32),
        in_specs=[VMEM],
        out_specs=VMEM,
        scratch_shapes=[pltpu.VMEM((count * size, 128), jnp.float32)] * (width // 128),
        compiler_params=params(),
        cost_estimate=cost(parts.size, 8 * parts.size),
    )(parts)


def add_product(total_ref, window, tap_ref, first):
    size = 512
    for low in range(0, total_ref.shape[1], size):
        lanes = slice(low, low + size)
        product = multiply_transposed(window, tap_ref[low : low + size, :])
        total_ref[:, lanes] = product if first else total_ref[:, lanes] + product


def input_gradient_kernel(
    windows_ref,
    grads_ref,
    east_ref,
    west_ref,
    up_near_ref,
    up_far_ref,
    down_near_ref,
    down_far_ref,
    kernel_ref,
    point_weight_ref,
    out_ref,
    total_ref,
    buffer_ref,
    semaphores,
    *row_refs,
):
    width = buffer_ref.shape[2]
    cols, rows, _ = out_ref.shape
    sources = [point_weight_ref] + [kernel_ref.at[tap] for tap in (1, 4, 7, 2, 5, 8, 0, 3, 6)]
    for at, tap_ref in enumerate(stream(sources, buffer_ref, semaphores)):
        side, i = divmod(at - 4, 3)
        lanes = slice(side * width, (side + 1) * width)
        if at == 0:
            window = grads_ref[:, width:]
        elif at < 4:
            window = windows_ref[:, (at - 1) * width : at * width]
        elif i == 0:
            window = jnp.concatenate([up_near_ref[:, lanes], up_far_ref[:, lanes]])
        elif i == 1:
            window = (east_ref, west_ref)[side][...]
        else:
            window = jnp.concatenate([down_far_ref[:, lanes], down_near_ref[:, lanes]])
        add_product(total_ref, window, tap_ref, at == 0)
    for block, row_ref in enumerate(row_refs):
        lanes = slice(128 * block, 128 * block + 128)
        row_ref[...] = total_ref[:, lanes]
        for col in range(cols):
            out_ref[col, :, lanes] = row_ref[pl.ds(col, rows, stride=cols), :].astype(out_ref.dtype)


def input_gradient(rows, windows, grads, east, west, side_rows, kernel, point_weight):
    pixels = grads.shape[0]
    in_width, width = point_weight.shape
    return pl.pallas_call(
        input_gradient_kernel,
        out_shape=like((pixels // rows, rows, in_width), jnp.bfloat16),
        in_specs=[VMEM] * 8 + [ANY] * 2,
        out_specs=VMEM,
        scratch_shapes=[pltpu.VMEM((pixels, in_width), jnp.float32)]
        + stream_scratch(in_width, width)
        + [pltpu.VMEM((pixels, 128), jnp.float32)] * (in_width // 128),
        compiler_params=params(60),
        cost_estimate=cost(20 * pixels * in_width * width, 40 * in_width * width),
    )(windows, grads, east, west, *side_rows, kernel, point_weight)


def shards(features, kernel, point_weight, project_weight, upstream, labels, class_weights):
    rows, cols, in_width = features.shape
    width = point_weight.shape[1]
    pixels = rows * cols
    place = jnp.stack([lax.axis_index("c"), lax.axis_index("y"), lax.axis_index("xh")])
    near = ATROUS_DILATION // rows
    far_pixels = (ATROUS_DILATION - near * rows) * cols
    tiles_over = ATROUS_DILATION // cols
    span = ATROUS_DILATION * cols

    flat, slices = channel_slices(features)
    below_near, below_far, above_near, above_far, level, point_pre = tap_products(
        flat, kernel, point_weight, far_pixels, slices
    )
    received = (
        shift_rows(below_near, -near),
        shift_rows(below_far, -(near + 1)),
        shift_rows(above_near, near),
        shift_rows(above_far, near + 1),
    )
    column_features = lax.all_to_all(slices, LAT, 0, 0).reshape(LAT_COUNT * pixels, -1)
    first_rows = FIRST_BANDS * pixels
    first_features, second_features = column_features[:first_rows], column_features[first_rows:]
    to_east, to_west, center = row_sum(level, received)
    from_east = shift_columns(to_west, -tiles_over)
    from_west = shift_columns(to_east, tiles_over)
    class_index = jnp.arange(3, dtype=jnp.int32)
    pixel_weight = jnp.sum(
        jnp.where(labels[..., None] == class_index, class_weights, 0.0), axis=-1
    ).reshape(-1, 1)
    head_out, grads, message, mine = head(
        rows,
        place,
        point_pre,
        center,
        from_east,
        from_west,
        project_weight,
        upstream.reshape(pixels, width),
        pixel_weight,
    )

    other = lax.ppermute(message, "xh", [(0, 1), (1, 0)])
    first_east = shift_columns(first_features, -tiles_over)
    first_west = shift_columns(first_features, tiles_over)
    east_grad = shift_columns(grads[:, :width], tiles_over)
    west_grad = shift_columns(grads[:, :width], -tiles_over)
    message, second_features = forward(
        grads, other, mine, (first_east, first_west, east_grad, west_grad), second_features
    )
    gathered = lax.all_to_all(message, "y", 0, 0)
    second_east = shift_columns(second_features, -tiles_over)
    second_west = shift_columns(second_features, tiles_over)

    kept, sent, windows = weight_terms(
        span,
        place,
        (column_features, first_east, second_east, first_west, second_west),
        gathered,
    )
    chunk = (10 * in_width + 2 * width) // (LAT_COUNT * LON_COUNT)
    chip_sum = pair_sum(kept, lax.ppermute(sent, "c", [(0, 1), (1, 0)]), chunk)
    up_near, up_far, down_near, down_far = side_slices(east_grad, west_grad, far_pixels)
    side_rows = (
        shift_rows(up_near, -near),
        shift_rows(up_far, -(near + 1)),
        shift_rows(down_near, near),
        shift_rows(down_far, near + 1),
    )
    pieces = lax.all_to_all(chip_sum, ("xl", "z"), 0, 0)

    weight_grads = interleave(lax.all_to_all(piece_sum(pieces, side_rows), LAT, 0, 0))
    input_grad = input_gradient(
        rows, windows, grads, east_grad, west_grad, side_rows, kernel, point_weight
    )

    head_tile = jnp.swapaxes(head_out, 0, 1)
    grad_tile = jnp.swapaxes(input_grad, 0, 1)
    return (head_tile, grad_tile, weight_grads)


def solution(mesh):
    split = Mesh(mesh.devices.reshape(tuple(AXIS_SIZES.values())), tuple(AXIS_SIZES))
    tile = P(LAT, LON, None)
    return jax.shard_map(
        shards,
        mesh=split,
        in_specs=(tile, P(), P(), P(), tile, P(LAT, LON), P()),
        out_specs=(tile, tile, P(LON, None)),
        check_vma=False,
    )
```
